512 devices in a mesh: ens: 16 (over z_lo, core), space: 32 (over y, x, z_hi).
Axes of the slice: x: 4, y: 4, z: 16 (z_hi: 2, z_lo: 8; z = z_hi * 8 + z_lo), core: 2. Of those that a mesh axis runs over, the one named last changes fastest.
Arguments:
- latents: bfloat16 [16, 16384, 1024], P('ens', 'space'), may hold values from -6 to 6
- w_mix: bfloat16 [1024, 1024], P('space'), may hold values from -0.1875 to 0.1875
- w_out: bfloat16 [1024, 16], replicated, may hold values from -0.1875 to 0.1875
- bias: float32 [16], replicated, may hold values from -3 to 3
- truth: float32 [16, 16384], P(None, 'space'), may hold values from -6 to 6
- area: float32 [16384], P('space'), may hold values from 0.25 to 4
Outputs:
- grad_latents: bfloat16 [16, 16384, 1024], P('ens', 'space')
- grad_mix: float32 [1024, 1024], P('space')
- grad_out: float32 [1024, 16], replicated
- grad_bias: float32 [16], replicated
- loss: float32 [], replicated
The draws below stay inside these ranges and needn't reach their ends.
All inputs are finite; a program needn't handle non-finite values.
Results may differ from the reference program's by a relative error of at most 0.0057.
The reference program's roundings to bfloat16 on the way count: a program that leaves them out, or rounds other values in their place, can miss the bound.
Values may be sent and summed in bfloat16 or wider, within the bound.
No kernel may reach another device: no remote copies, remote signals or barrier semaphores. Data moves between devices by JAX's collectives and lax.ppermute only.
A program may use at most 64 MiB of HBM per device.

```python
import math
import jax
import jax.numpy as jnp
from jax import lax

M = 16
C = 1024
F = 16
NP = 16384


def with_spikes(result, key, source, target, shards_of, factor):
    owner, partner = [(jnp.arange(result.shape[position]) // (result.shape[position] // shards_of)).reshape([-1 if axis == position else 1 for axis in range(result.ndim)]) for position in (source, target)]
    chosen = jax.random.permutation(key, shards_of)[partner]
    strong = (owner == chosen) | (owner == (partner + shards_of // 2) % shards_of)
    return jnp.where(strong, factor * result, result)


def block_levels(key, shape, shards, low, top_value):
    gain = 1.0
    for position, parts in shards:
        heights = jax.random.uniform(jax.random.fold_in(jax.random.fold_in(key, 6), position), (parts,), jnp.float32, low / len(shards), top_value / len(shards))
        gain = gain * jnp.repeat(jnp.exp(heights), shape[position] // parts).reshape((-1,) + (1,) * (len(shape) - 1 - position))
    return gain


def scatter_about(rng, shape, width, limit, split=(), kind=jnp.bfloat16):
    result = jax.random.normal(rng, shape, jnp.float32) * width
    if len(split) > 0:
        result = block_levels(rng, shape, split, -0.22, 0.18) * result
    return jnp.clip(result, min=-limit, max=limit).astype(kind)


def heavy_noise(stream_key, extent, scale, limit, split, heavy, kind=jnp.bfloat16):
    values = scale * jax.random.normal(stream_key, extent, jnp.float32)
    if split:
        values = values * block_levels(stream_key, extent, split, -0.22, 0.18)
    return jnp.clip(with_spikes(values, jax.random.fold_in(stream_key, 3), *heavy), -limit, limit).astype(kind)


def setup_inputs(seed: int = 0) -> dict:
    key_of = jax.random.split(jax.random.key(seed), 7)
    return {
        "latents": heavy_noise(key_of[0], (M, NP, C), 1.0, 6.0, ((0, 16), (1, 32)), (1, 2, 32, 2.75)),
        "w_mix": scatter_about(key_of[1], (C, C), C ** -0.5, 0.1875, ((0, 32),)),
        "w_out": scatter_about(key_of[2], (C, F), C ** -0.5, 0.1875),
        "bias": scatter_about(key_of[3], (F,), 0.5, 3.0, (), jnp.float32),
        "truth": scatter_about(key_of[4], (F, NP), 1.0, 6.0, ((1, 32),), jnp.float32),
        "area": jnp.clip(jnp.exp(math.log(4.0) - 2.7725887 * jax.random.uniform(key_of[5], (NP,), jnp.float32) ** block_levels(key_of[5], (NP,), ((0, 32),), -0.2, 0.2)), 0.25, 4.0),
    }


smoothing = 0.1

def pairwise_terms(chosen, members, observed, weights_pt):
    count_all = float(M)
    differ = chosen[:, :, None, :] - members[:, None, :, :]
    smooth = jnp.sqrt(differ * differ + smoothing * smoothing)
    slopes = differ / smooth
    to_truth = chosen - observed[:, None, :]
    absolute = jnp.sqrt(to_truth * to_truth + smoothing * smoothing)
    pairs_norm = count_all * (count_all - 1.0)
    member_gradient = weights_pt * (to_truth / absolute / count_all - lax.optimization_barrier(jnp.sum(slopes, axis=2)) / pairs_norm)
    partial_loss = jnp.sum(weights_pt * (absolute / count_all - (lax.optimization_barrier(jnp.sum(smooth, axis=2)) - smoothing) / (2.0 * pairs_norm)))
    return (member_gradient, partial_loss)

def reference(latents, w_mix, w_out, bias, truth, area):

    def forward_apply(member_z):
        pre_act = jnp.dot(member_z, w_mix, preferred_element_type=jnp.float32)
        hidden = jax.nn.gelu(pre_act).astype(jnp.bfloat16)
        return lax.dot_general(w_out, hidden, (((0,), (1,)), ((), ())), preferred_element_type=jnp.float32) + bias[:, None]
    predicted_fields = jnp.transpose(lax.map(forward_apply, latents), (1, 0, 2))
    member_gradient, overall_loss = pairwise_terms(predicted_fields, predicted_fields, truth, area)
    grad_bf = member_gradient.astype(jnp.bfloat16)

    def backward(inputs):
        member_z, member_g = inputs
        pre_act = jnp.dot(member_z, w_mix, preferred_element_type=jnp.float32)
        hidden = jax.nn.gelu(pre_act).astype(jnp.bfloat16)
        head_term = lax.dot_general(hidden, member_g, (((0,), (1,)), ((), ())), preferred_element_type=jnp.float32)
        grad_hidden = lax.dot_general(member_g, w_out, (((0,), (1,)), ((), ())), preferred_element_type=jnp.float32)
        unused_value, pullback = jax.vjp(jax.nn.gelu, pre_act)
        grad_pre = pullback(grad_hidden)[0].astype(jnp.bfloat16)
        grad_rows = lax.dot_general(grad_pre, w_mix, (((1,), (1,)), ((), ())), preferred_element_type=jnp.float32)
        mix_term = lax.dot_general(member_z, grad_pre, (((0,), (0,)), ((), ())), preferred_element_type=jnp.float32)
        return (grad_rows.astype(jnp.bfloat16), mix_term, head_term)
    grad_latents, mix_terms, head_terms = lax.map(backward, (latents, jnp.transpose(grad_bf, (1, 0, 2))))
    grad_mix = lax.optimization_barrier(jnp.sum(mix_terms, axis=0))
    grad_out = lax.optimization_barrier(jnp.sum(head_terms, axis=0))
    grad_bias = lax.optimization_barrier(jnp.sum(grad_bf.astype(jnp.float32), axis=(1, 2)))
    loss = overall_loss / NP
    return (grad_latents, grad_mix, grad_out, grad_bias, loss)
```

```python
import jax
import jax.numpy as jnp
from jax import lax
from jax.sharding import Mesh
from jax.sharding import PartitionSpec as P

M = 16
smoothing = 0.1
Z, CORES, Y, X, H = 8, 2, 4, 4, 2
ENS, SPACE, PLANE = ("z", "c"), ("y", "x", "h"), ("y", "x")
f32, bf16 = jnp.float32, jnp.bfloat16
SWAP = ((0, 1), (1, 0))
MIRROR = tuple((z * H + h, (Z - 1 - z) * H + 1 - h) for z in range(Z) for h in range(H))


def split3(values):
    first = lax.reduce_precision(values, 8, 7)
    second = lax.reduce_precision(values - first, 8, 7)
    third = values - first - second
    return jnp.concatenate([first, second, third]).astype(bf16)


def scalar_rows(values, width):
    terms = split3(values)
    row = jnp.pad(terms, (0, width - terms.shape[0]))
    return jnp.pad(row[None, :], ((0, 7), (0, 0)))


def scalars_of(row, count):
    return row[:count] + row[count : 2 * count] + row[2 * count : 3 * count]


def pairwise(chosen, members, observed, weights):
    count_all = float(M)
    differ = chosen[:, None] - members[None]
    smooth = jnp.sqrt(differ * differ + smoothing * smoothing)
    slopes = differ / smooth
    to_truth = chosen - observed
    absolute = jnp.sqrt(to_truth * to_truth + smoothing * smoothing)
    pairs_norm = count_all * (count_all - 1.0)
    gradient = weights * (
        to_truth / absolute / count_all - jnp.sum(slopes, axis=1) / pairs_norm
    )
    partial = jnp.sum(
        weights
        * (absolute / count_all - (jnp.sum(smooth, axis=1) - smoothing) / (2.0 * pairs_norm))
    )
    return gradient, partial


def dot(a, b, ca, cb):
    return lax.dot_general(a, b, (((ca,), (cb,)), ((), ())), preferred_element_type=f32)


def body(latents, w_mix, w_out, bias, truth, area):
    core = lax.axis_index("c")
    first = core == 0
    half_ring = lax.axis_index("h")
    points, width = latents.shape[1], latents.shape[2]
    fields = w_out.shape[1]
    rows = w_mix.shape[0]
    half, ph = width // 2, points // 2
    lat = latents[0]

    def pick(a, b):
        return jnp.where(first, a, b)

    def ordered(own, other, axis):
        return pick(
            jnp.concatenate([own, other], axis), jnp.concatenate([other, own], axis)
        )

    mine = pick(w_mix[:, :half], w_mix[:, half:])
    far = lax.ppermute(mine, ("z", "h"), MIRROR)
    near = jnp.where(
        half_ring == 0, jnp.concatenate([mine, far], 0), jnp.concatenate([far, mine], 0)
    )
    sent = jnp.broadcast_to(near[None], (Y * X, H * rows, half))
    w_own = lax.all_to_all(sent, PLANE, 0, 0, tiled=True).reshape(width, half)
    w_oth = lax.ppermute(w_own, "c", SWAP)
    out_own = pick(w_out[:half], w_out[half:])
    out_oth = pick(w_out[half:], w_out[:half])

    pre_own = dot(lat, w_own, 1, 0)
    hid_own = jax.nn.gelu(pre_own).astype(bf16)
    pre_oth = dot(lat, w_oth, 1, 0)
    hid_oth = jax.nn.gelu(pre_oth).astype(bf16)
    forecast = dot(out_own, hid_own, 0, 1) + dot(out_oth, hid_oth, 0, 1) + bias[:, None]

    fc_own = pick(forecast[:, :ph], forecast[:, ph:])
    fc_oth = lax.ppermute(pick(forecast[:, ph:], forecast[:, :ph]), "c", SWAP)
    chosen = jnp.stack([fc_own, fc_oth])
    members = lax.all_to_all(
        jnp.broadcast_to(chosen.reshape(1, 2 * fields, ph), (Z, 2 * fields, ph)),
        "z", 0, 0, tiled=True,
    ).reshape(M, fields, ph)
    observed = pick(truth[:, :ph], truth[:, ph:])
    weights = pick(area[:ph], area[ph:])
    gradient, partial = pairwise(chosen, members, observed, weights)
    grad_bf = gradient.astype(bf16)
    g_back = lax.ppermute(grad_bf[1], "c", SWAP)
    g = ordered(grad_bf[0], g_back, 1)
    sums = jnp.concatenate(
        [jnp.sum(grad_bf.astype(f32), axis=(0, 2)), partial.reshape(1)]
    )

    def backward(pre, out):
        unused_value, pullback = jax.vjp(jax.nn.gelu, pre)
        return pullback(dot(g, out, 0, 1))[0].astype(bf16)

    gp_oth = backward(pre_oth, out_oth)
    mix_oth = dot(lat, gp_oth, 0, 0)
    mix_in = lax.ppermute(mix_oth.astype(bf16), "c", SWAP)
    head_oth = jnp.concatenate(
        [dot(g, hid_oth, 1, 0).astype(bf16), scalar_rows(sums, half)], 0
    )
    head_in = lax.ppermute(head_oth, "c", SWAP).astype(f32)
    gp_own = backward(pre_own, out_own)
    mix = dot(lat, gp_own, 0, 0) + mix_in.astype(f32)
    head = dot(g, hid_own, 1, 0) + head_in[:fields]
    sums = sums + scalars_of(head_in[fields], fields + 1)
    grad_rows = dot(gp_own, w_own, 1, 1) + dot(gp_oth, w_oth, 1, 1)
    grad_latents = grad_rows.astype(bf16)[None]

    extra = jnp.concatenate([head.astype(bf16), scalar_rows(sums, half)], 0)
    sent = jnp.concatenate(
        [
            mix.astype(bf16).reshape(Y * X, H * rows, half),
            jnp.broadcast_to(extra[None], (Y * X,) + extra.shape),
        ],
        1,
    )
    got = jnp.sum(lax.all_to_all(sent, PLANE, 0, 0, tiled=True).astype(f32), axis=0)
    mix, head = got[: H * rows], got[H * rows : H * rows + fields]
    sums = scalars_of(got[H * rows + fields], fields + 1)

    per, hper = rows // Z, fields // Z
    tail = jnp.broadcast_to(scalar_rows(sums, half)[:1][None], (H * Z, 1, half))
    head = jnp.broadcast_to(
        head.astype(bf16).reshape(1, Z, hper, half), (H, Z, hper, half)
    ).reshape(H * Z, hper, half)
    sent = jnp.concatenate(
        [mix.astype(bf16).reshape(H * Z, per, half), head, tail, jnp.zeros_like(tail)], 1
    )
    got = jnp.sum(lax.all_to_all(sent, ("h", "z"), 0, 0, tiled=True).astype(f32), axis=0)
    sums = scalars_of(got[per + hper], fields + 1)
    sent = jnp.broadcast_to(got[None].astype(bf16), (Z,) + got.shape)
    got = lax.all_to_all(sent, "z", 0, 0, tiled=True)
    own = jnp.concatenate(
        [got[:, :per].reshape(rows, half), got[:, per : per + hper].reshape(fields, half)], 0
    )
    other = lax.ppermute(own, "c", SWAP)
    whole = ordered(own, other, 1).astype(f32)
    grad_mix, grad_out = whole[:rows], whole[rows:].T
    loss = sums[fields] / (points * Y * X * H)
    return grad_latents, grad_mix, grad_out, sums[:fields], loss


def solution(mesh):
    fine = Mesh(mesh.devices.reshape(Z, CORES, Y, X, H), ("z", "c", "y", "x", "h"))
    in_specs = (P(ENS, SPACE, None), P(SPACE, None), P(), P(), P(None, SPACE), P(SPACE))
    out_specs = (P(ENS, SPACE, None), P(SPACE, None), P(), P(), P())
    return jax.shard_map(
        body, mesh=fine, in_specs=in_specs, out_specs=out_specs, check_vma=False
    )
```

```python
import jax
import jax.numpy as jnp
from jax import lax
from jax.sharding import Mesh
from jax.sharding import PartitionSpec as P

M = 16
smoothing = 0.1
FAR, NEAR, CORES, Y, X, H = 2, 4, 2, 4, 4, 2
Z = FAR * NEAR
RING = ("far", "near")
ENS, SPACE, PLANE = ("far", "near", "c"), ("y", "x", "h"), ("y", "x")
f32, bf16 = jnp.float32, jnp.bfloat16
SWAP = ((0, 1), (1, 0))
ACROSS = tuple((far * H + h, (1 - far) * H + 1 - h) for far in range(FAR) for h in range(H))


def split3(values):
    first = lax.reduce_precision(values, 8, 7)
    second = lax.reduce_precision(values - first, 8, 7)
    third = values - first - second
    return jnp.concatenate([first, second, third]).astype(bf16)


def scalar_rows(values, width):
    terms = split3(values)
    row = jnp.pad(terms, (0, width - terms.shape[0]))
    return jnp.pad(row[None, :], ((0, 7), (0, 0)))


def scalars_of(row, count):
    return row[:count] + row[count : 2 * count] + row[2 * count : 3 * count]


def member_sums(chosen, members):
    differ = chosen[None] - members
    smooth = jnp.sqrt(differ * differ + smoothing * smoothing)
    return jnp.sum(differ / smooth, axis=0), jnp.sum(smooth, axis=0)


def all_to_all(x, axes):
    return lax.all_to_all(x, axes, 0, 0, tiled=True)


def copies(x, count):
    return jnp.broadcast_to(x[None], (count,) + x.shape)


def dot(a, b, ca, cb):
    return lax.dot_general(a, b, (((ca,), (cb,)), ((), ())), preferred_element_type=f32)


def body(latents, w_mix, w_out, bias, truth, area):
    core = lax.axis_index("c")
    first = core == 0
    half_ring = lax.axis_index("h")
    points, width = latents.shape[1], latents.shape[2]
    fields = w_out.shape[1]
    rows = w_mix.shape[0]
    half = width // 2
    lat = latents[0]

    def pick(a, b):
        return jnp.where(first, a, b)

    def ordered(own, other, axis):
        return pick(
            jnp.concatenate([own, other], axis), jnp.concatenate([other, own], axis)
        )

    mine = pick(w_mix[:, :half], w_mix[:, half:])
    far = lax.ppermute(mine, ("far", "h"), ACROSS)
    near = jnp.where(
        half_ring == 0, jnp.concatenate([mine, far], 0), jnp.concatenate([far, mine], 0)
    )
    sent = jnp.broadcast_to(near[None], (Y * X, H * rows, half))
    w_own = lax.all_to_all(sent, PLANE, 0, 0, tiled=True).reshape(width, half)
    w_oth = lax.ppermute(w_own, "c", SWAP)
    out_own = pick(w_out[:half], w_out[half:])
    out_oth = pick(w_out[half:], w_out[:half])

    pre_own = dot(lat, w_own, 1, 0)
    hid_own = jax.nn.gelu(pre_own).astype(bf16)
    pre_oth = dot(lat, w_oth, 1, 0)
    hid_oth = jax.nn.gelu(pre_oth).astype(bf16)
    forecast = dot(out_own, hid_own, 0, 1) + dot(out_oth, hid_oth, 0, 1) + bias[:, None]

    sent = jnp.broadcast_to(forecast[None], (Z, fields, points))
    members = lax.all_to_all(sent, RING, 0, 0, tiled=True)
    others = lax.ppermute(members, "c", SWAP)
    slope, smooth = member_sums(forecast, members)
    slope_oth, smooth_oth = member_sums(forecast, others)
    slope, smooth = slope + slope_oth, smooth + smooth_oth
    count_all = float(M)
    pairs_norm = count_all * (count_all - 1.0)
    to_truth = forecast - truth
    absolute = jnp.sqrt(to_truth * to_truth + smoothing * smoothing)
    g = (area * (to_truth / absolute / count_all - slope / pairs_norm)).astype(bf16)
    partial = jnp.sum(
        area * (absolute / count_all - (smooth - smoothing) / (2.0 * pairs_norm))
    )
    sums = jnp.concatenate([jnp.sum(g.astype(f32), axis=1), partial.reshape(1)])

    def backward(pre, out):
        unused_value, pullback = jax.vjp(jax.nn.gelu, pre)
        return pullback(dot(g, out, 0, 1))[0].astype(bf16)

    gp_oth = backward(pre_oth, out_oth)
    mix_oth = dot(lat, gp_oth, 0, 0)
    mix_in = lax.ppermute(mix_oth.astype(bf16), "c", SWAP)
    head_oth = jnp.concatenate(
        [dot(g, hid_oth, 1, 0).astype(bf16), scalar_rows(sums, half)], 0
    )
    head_in = lax.ppermute(head_oth, "c", SWAP).astype(f32)
    gp_own = backward(pre_own, out_own)
    mix = dot(lat, gp_own, 0, 0) + mix_in.astype(f32)
    head = dot(g, hid_own, 1, 0) + head_in[:fields]
    sums = sums + scalars_of(head_in[fields], fields + 1)
    grad_rows = dot(gp_own, w_own, 1, 1) + dot(gp_oth, w_oth, 1, 1)
    grad_latents = grad_rows.astype(bf16)[None]

    extra = jnp.concatenate([head.astype(bf16), scalar_rows(sums, half)], 0)
    sent = jnp.concatenate(
        [
            mix.astype(bf16).reshape(Y * X, H * rows, half),
            jnp.broadcast_to(extra[None], (Y * X,) + extra.shape),
        ],
        1,
    )
    got = jnp.sum(lax.all_to_all(sent, PLANE, 0, 0, tiled=True).astype(f32), axis=0)

    part, hpart = rows // NEAR, fields // NEAR
    sums = scalars_of(got[H * rows + fields], fields + 1)
    mix = got[: H * rows].astype(bf16).reshape(H, NEAR, part, half)
    head = got[H * rows : H * rows + fields].astype(bf16).reshape(NEAR, hpart, half)
    tail = copies(scalar_rows(sums, half)[: 8 - hpart], NEAR)
    sent = jnp.concatenate([mix[0], mix[1], head, tail], 1)
    got = jnp.sum(all_to_all(sent, "near").astype(f32), axis=0)
    sums = scalars_of(got[H * part + hpart], fields + 1)
    mix = got[: H * part].astype(bf16).reshape(H, part, half)
    head = got[H * part : H * part + hpart].astype(bf16)
    tail = jnp.concatenate([head, scalar_rows(sums, half)[: 8 - hpart]], 0)
    sent = jnp.concatenate([mix, copies(tail, H)], 1)
    sent = jnp.broadcast_to(sent[:, None], (H, FAR, part + 8, half))
    got = jnp.sum(
        all_to_all(sent.reshape(H * FAR, part + 8, half), ("h", "far")).astype(f32), axis=0
    )
    sums = scalars_of(got[part + hpart], fields + 1)

    got = all_to_all(copies(got.astype(bf16), NEAR * CORES), ("near", "c")).astype(f32)
    got = got.reshape(NEAR, CORES, part + 8, half)
    grad_mix = jnp.concatenate([got[:, 0, :part], got[:, 1, :part]], 2).reshape(rows, width)
    head = got[:, :, part : part + hpart]
    grad_out = jnp.concatenate([head[:, 0], head[:, 1]], 2).reshape(fields, width).T
    loss = sums[fields] / (points * Y * X * H)
    return grad_latents, grad_mix, grad_out, sums[:fields], loss


def solution(mesh):
    shape = (FAR, NEAR, CORES, Y, X, H)
    fine = Mesh(mesh.devices.reshape(shape), ("far", "near", "c", "y", "x", "h"))
    in_specs = (P(ENS, SPACE, None), P(SPACE, None), P(), P(), P(None, SPACE), P(SPACE))
    out_specs = (P(ENS, SPACE, None), P(SPACE, None), P(), P(), P())
    return jax.shard_map(
        body, mesh=fine, in_specs=in_specs, out_specs=out_specs, check_vma=False
    )
```

```python
import jax
import jax.numpy as jnp
from jax import lax
from jax.sharding import Mesh
from jax.sharding import PartitionSpec as P

M = 16
smoothing = 0.1
FAR, NEAR, CORES, Y, X, H = 2, 4, 2, 4, 4, 2
Z = FAR * NEAR
RING = ("far", "near")
ENS, SPACE, PLANE = ("far", "near", "c"), ("y", "x", "h"), ("y", "x")
f32, bf16 = jnp.float32, jnp.bfloat16
SWAP = ((0, 1), (1, 0))
ACROSS = tuple((far * H + h, (1 - far) * H + 1 - h) for far in range(FAR) for h in range(H))


def scalar_rows(values, width, count):
    first = lax.reduce_precision(values, 8, 7)
    second = lax.reduce_precision(values - first, 8, 7)
    third = values - first - second
    terms = jnp.concatenate([first, second, third]).astype(bf16)
    return jnp.pad(terms[None], ((0, count - 1), (0, width - terms.shape[0])))


def scalars_of(row, count):
    return row[:count] + row[count : 2 * count] + row[2 * count : 3 * count]


def member_sums(chosen, members):
    differ = chosen[None] - members
    smooth = jnp.sqrt(differ * differ + smoothing * smoothing)
    return jnp.sum(differ / smooth, axis=0), jnp.sum(smooth, axis=0)


def pairwise(chosen, members, others, observed, weights):
    slope, smooth = member_sums(chosen, members)
    slope_oth, smooth_oth = member_sums(chosen, others)
    slope, smooth = slope + slope_oth, smooth + smooth_oth
    count_all = float(M)
    pairs_norm = count_all * (count_all - 1.0)
    to_truth = chosen - observed
    absolute = jnp.sqrt(to_truth * to_truth + smoothing * smoothing)
    gradient = weights * (to_truth / absolute / count_all - slope / pairs_norm)
    partial = jnp.sum(
        weights * (absolute / count_all - (smooth - smoothing) / (2.0 * pairs_norm))
    )
    return gradient.astype(bf16), partial


def all_to_all(x, axes):
    return lax.all_to_all(x, axes, 0, 0, tiled=True)


def copies(x, count):
    return jnp.broadcast_to(x[None], (count,) + x.shape)


def dot(a, b, ca, cb):
    return lax.dot_general(a, b, (((ca,), (cb,)), ((), ())), preferred_element_type=f32)


def body(latents, w_mix, w_out, bias, truth, area):
    first = lax.axis_index("c") == 0
    low = lax.axis_index("h") == 0
    points, width = latents.shape[1], latents.shape[2]
    fields = w_out.shape[1]
    rows = w_mix.shape[0]
    half = width // 2

    def pick(a, b):
        return jnp.where(first, a, b)

    mine = pick(w_mix[:, :half], w_mix[:, half:])
    far = lax.ppermute(mine, ("far", "h"), ACROSS)
    near = jnp.where(low, jnp.concatenate([mine, far], 0), jnp.concatenate([far, mine], 0))
    w_own = all_to_all(copies(near, Y * X), PLANE).reshape(width, half)
    out_own = pick(w_out[:half], w_out[half:])

    lat_own = latents[0]
    lat_oth = lax.ppermute(lat_own, "c", SWAP)
    pre_own = dot(lat_own, w_own, 1, 0)
    hid_own = jax.nn.gelu(pre_own).astype(bf16)
    pre_oth = dot(lat_oth, w_own, 1, 0)
    hid_oth = jax.nn.gelu(pre_oth).astype(bf16)
    fc_own, fc_oth = dot(out_own, hid_own, 0, 1), dot(out_own, hid_oth, 0, 1)

    rest = lax.ppermute(jnp.stack([fc_oth, fc_own]), "c", SWAP)
    fc_own = fc_own + rest[0] + bias[:, None]
    fc_oth = fc_oth + rest[1] + bias[:, None]
    members = all_to_all(copies(fc_own, Z), RING)
    others = lax.ppermute(members, "c", SWAP)
    g_own, partial = pairwise(fc_own, members, others, truth, area)
    g_oth, unused_partial = pairwise(fc_oth, members, others, truth, area)
    sums = jnp.concatenate([jnp.sum(g_own.astype(f32), axis=1), partial.reshape(1)])

    def backward(pre, g):
        unused_value, pullback = jax.vjp(jax.nn.gelu, pre)
        return pullback(dot(g, out_own, 0, 1))[0].astype(bf16)

    gp_own, gp_oth = backward(pre_own, g_own), backward(pre_oth, g_oth)
    mix = (dot(lat_own, gp_own, 0, 0) + dot(lat_oth, gp_oth, 0, 0)).astype(bf16)
    head = dot(g_own, hid_own, 1, 0) + dot(g_oth, hid_oth, 1, 0)

    extra = jnp.concatenate([head.astype(bf16), scalar_rows(sums, half, 8)], 0)
    sent = jnp.concatenate([mix.reshape(Y * X, H * rows, half), copies(extra, Y * X)], 1)
    got = jnp.sum(all_to_all(sent, PLANE).astype(f32), axis=0)

    piece, hpiece = rows // NEAR, fields // NEAR
    sums = scalars_of(got[H * rows + fields], fields + 1)
    mix = got[: H * rows].astype(bf16).reshape(H, NEAR, piece, half)
    head = got[H * rows : H * rows + fields].astype(bf16).reshape(NEAR, hpiece, half)
    tail = copies(scalar_rows(sums, half, 8 - hpiece), NEAR)
    sent = jnp.concatenate([mix[0], mix[1], head, tail], 1)
    got = jnp.sum(all_to_all(sent, "near").astype(f32), axis=0)
    sums = scalars_of(got[H * piece + hpiece], fields + 1)
    mix = got[: H * piece].astype(bf16).reshape(H, piece, half)
    head = got[H * piece : H * piece + hpiece].astype(bf16)
    tail = jnp.concatenate([head, scalar_rows(sums, half, 8 - hpiece)], 0)
    sent = jnp.concatenate([mix, copies(tail, H)], 1)
    sent = jnp.broadcast_to(sent[:, None], (H, FAR, piece + 8, half))
    sent = sent.reshape(H * FAR, piece + 8, half)
    got = jnp.sum(all_to_all(sent, ("h", "far")).astype(f32), axis=0)

    sums = scalars_of(got[piece + hpiece], fields + 1)
    sent = jnp.concatenate(
        [got[: piece + hpiece].astype(bf16), scalar_rows(sums, half, 8 - hpiece)], 0
    )
    got = all_to_all(copies(sent, NEAR * CORES), ("near", "c")).astype(f32)
    got = got.reshape(NEAR, CORES, piece + 8, half)
    grad_mix = jnp.concatenate([got[:, 0, :piece], got[:, 1, :piece]], 2).reshape(rows, width)
    head = got[:, :, piece : piece + hpiece]
    grad_out = jnp.concatenate([head[:, 0], head[:, 1]], 2).reshape(fields, width).T
    sums = scalars_of(got[0, 0, piece + hpiece] + got[0, 1, piece + hpiece], fields + 1)
    loss = sums[fields] / (points * Y * X * H)

    grad_rows = lax.ppermute(dot(gp_oth, w_own, 1, 1).astype(bf16), "c", SWAP)
    grad_latents = (dot(gp_own, w_own, 1, 1) + grad_rows.astype(f32)).astype(bf16)[None]
    return grad_latents, grad_mix, grad_out, sums[:fields], loss


def solution(mesh):
    shape = (FAR, NEAR, CORES, Y, X, H)
    fine = Mesh(mesh.devices.reshape(shape), ("far", "near", "c", "y", "x", "h"))
    in_specs = (P(ENS, SPACE, None), P(SPACE, None), P(), P(), P(None, SPACE), P(SPACE))
    out_specs = (P(ENS, SPACE, None), P(SPACE, None), P(), P(), P())
    return jax.shard_map(
        body, mesh=fine, in_specs=in_specs, out_specs=out_specs, check_vma=False
    )
```

```python
import functools

import jax
import jax.numpy as jnp
from jax import lax
from jax.experimental import pallas as pl
from jax.experimental.pallas import tpu as pltpu
from jax.sharding import Mesh
from jax.sharding import PartitionSpec as P

M = 16
smoothing = 0.1
FAR, NEAR, CORES, Y, X, H = 2, 4, 2, 4, 4, 2
Z = FAR * NEAR
RING = ("far", "near")
ENS, SPACE, PLANE = ("far", "near", "c"), ("y", "x", "h"), ("y", "x")
f32, bf16 = jnp.float32, jnp.bfloat16
SWAP = ((0, 1), (1, 0))
ACROSS = tuple((far * H + h, (1 - far) * H + 1 - h) for far in range(FAR) for h in range(H))


LANES = 128


def split_row(values, width):
    first = values.astype(bf16).astype(f32)
    second = (values - first).astype(bf16).astype(f32)
    third = values - first - second
    return jnp.concatenate(
        [first, second, third, jnp.zeros((1, width - 3 * LANES), f32)], 1
    )


def joined_row(row):
    return row[:, :LANES] + row[:, LANES : 2 * LANES] + row[:, 2 * LANES : 3 * LANES]


def total(ref):
    result = ref[0].astype(f32)
    for k in range(1, ref.shape[0]):
        result = result + ref[k].astype(f32)
    return result


def call(kernel, shapes, operands, scratch=(), flops=0, through=False):
    vmem = pl.BlockSpec(memory_space=pltpu.VMEM)
    many = isinstance(shapes, list)
    size = sum(o.size * o.dtype.itemsize for o in operands)
    in_specs = [vmem] * len(operands)
    out_specs = [vmem] * len(shapes) if many else vmem
    aliases = {}
    if through:
        in_specs[-1] = out_specs[-1] = pl.BlockSpec(memory_space=pl.ANY)
        aliases = {len(operands) - 1: len(shapes) - 1}
    return pl.pallas_call(
        kernel,
        out_shape=shapes,
        in_specs=in_specs,
        out_specs=out_specs,
        input_output_aliases=aliases,
        scratch_shapes=list(scratch),
        compiler_params=pltpu.CompilerParams(vmem_limit_bytes=40 << 20),
        cost_estimate=pl.CostEstimate(flops=flops, bytes_accessed=size, transcendentals=0),
    )(*operands)


def gelu_slope(x):
    scale = 0.7978845608028654
    square = x * x
    t = jnp.tanh(scale * x * (1.0 + 0.044715 * square))
    return 0.5 * (1.0 + t) + (0.5 * scale) * x * (1.0 - t * t) * (1.0 + 0.134145 * square)


def backward_kernel(
    g_own, g_oth, terms, out, pre_own, pre_oth, hid_own, hid_oth, lat_own, lat_oth,
    gp_own, gp_oth, sent,
):
    peers, rows = sent.shape[0], lat_own.shape[1] // sent.shape[0]
    fields, half = out.shape
    for g, pre, gp in ((g_own, pre_own, gp_own), (g_oth, pre_oth, gp_oth)):
        for k in range(0, pre.shape[0], 128):
            hidden = dot(g[:, k : k + 128], out[...], 0, 0)
            gp[k : k + 128] = (hidden * gelu_slope(pre[k : k + 128])).astype(bf16)
    step = 4
    for k in range(0, peers, step):
        columns = slice(k * rows, (k + step) * rows)
        mix = dot(lat_own[:, columns], gp_own[...], 0, 0)
        mix = mix + dot(lat_oth[:, columns], gp_oth[...], 0, 0)
        sent[k : k + step, :rows] = mix.astype(bf16).reshape(step, rows, half)

    head = dot(g_own[...], hid_own[...], 1, 0) + dot(g_oth[...], hid_oth[...], 1, 0)
    sums = jnp.sum(g_own[...].astype(f32), axis=1, keepdims=True)
    lane = lax.broadcasted_iota(jnp.int32, (fields, LANES), 1)
    field = lax.broadcasted_iota(jnp.int32, (fields, LANES), 0)
    values = jnp.sum(jnp.where(lane == field, sums, 0.0), axis=0, keepdims=True)
    loss = jnp.sum(jnp.sum(terms[...], axis=1, keepdims=True), axis=0, keepdims=True)
    values = jnp.where(lane[:1] == fields, loss, values)
    tail = jnp.where(
        lax.broadcasted_iota(jnp.int32, (16, half), 0) == 0, split_row(values, half), 0.0
    )
    for k in range(peers):
        sent[k, rows : rows + fields] = head.astype(bf16)
        sent[k, rows + fields :] = tail.astype(bf16)


def pack(block, mix, head, values):
    start = 0
    for part in (*mix, head, split_row(values, block.shape[1])):
        block[start : start + part.shape[0]] = part
        start += part.shape[0]
    block[start:] = jnp.zeros((block.shape[0] - start, block.shape[1]), f32)
    return block[...].astype(bf16)


def neighbour_kernel(got, unused_in, sent, unused_out, block):
    rows, fields = got.shape[1] - 32, 16
    piece, hpiece = rows // H // NEAR, fields // NEAR
    whole = total(got)
    values = joined_row(whole[rows + fields : rows + fields + 1])
    for n in range(NEAR):
        mix = [
            whole[h * NEAR * piece + n * piece : h * NEAR * piece + (n + 1) * piece]
            for h in range(H)
        ]
        head = whole[rows + n * hpiece : rows + (n + 1) * hpiece]
        sent[n] = pack(block, mix, head, values)


def across_kernel(piece, hpiece, got, sent, block):
    whole = total(got)
    start = H * piece + hpiece
    values = joined_row(whole[start : start + 1])
    for h in range(H):
        mix = whole[h * piece : (h + 1) * piece]
        packed = pack(block, [mix], whole[H * piece : start], values)
        for far in range(FAR):
            sent[h * FAR + far] = packed


def gather_kernel(piece, hpiece, got, sent, block):
    whole = total(got)
    start = piece + hpiece
    values = joined_row(whole[start : start + 1])
    packed = pack(block, [whole[:piece]], whole[piece:start], values)
    for k in range(NEAR * CORES):
        sent[k] = packed


def assemble_kernel(count, got, mix, head, bias, loss):
    half = got.shape[2]
    piece, hpiece = mix.shape[0] // NEAR, head.shape[0] // NEAR
    for n in range(NEAR):
        for c in range(CORES):
            block = got[n * CORES + c].astype(f32)
            columns = slice(c * half, (c + 1) * half)
            mix[n * piece : (n + 1) * piece, columns] = block[:piece]
            head[n * hpiece : (n + 1) * hpiece, columns] = block[piece : piece + hpiece]
            if n == 0:
                row = joined_row(block[piece + hpiece : piece + hpiece + 1])
                values = row if c == 0 else values + row
    fields = head.shape[0]
    bias[...] = values[:, :fields]
    loss[...] = values[:, fields : fields + 1] / count


def member_sums(chosen, members):
    differ = chosen[None] - members
    smooth = jnp.sqrt(differ * differ + smoothing * smoothing)
    return jnp.sum(differ / smooth, axis=0), jnp.sum(smooth, axis=0)


def pairwise(chosen, members, others, observed, weights):
    slope, smooth = member_sums(chosen, members)
    slope_oth, smooth_oth = member_sums(chosen, others)
    slope, smooth = slope + slope_oth, smooth + smooth_oth
    count_all = float(M)
    pairs_norm = count_all * (count_all - 1.0)
    to_truth = chosen - observed
    absolute = jnp.sqrt(to_truth * to_truth + smoothing * smoothing)
    gradient = weights * (to_truth / absolute / count_all - slope / pairs_norm)
    terms = weights * (absolute / count_all - (smooth - smoothing) / (2.0 * pairs_norm))
    return gradient.astype(bf16), terms


def all_to_all(x, axes):
    return lax.all_to_all(x, axes, 0, 0, tiled=True)


def copies(x, count):
    return jnp.broadcast_to(x[None], (count,) + x.shape)


def dot(a, b, ca, cb):
    return lax.dot_general(a, b, (((ca,), (cb,)), ((), ())), preferred_element_type=f32)


def body(latents, w_mix, w_out, bias, truth, area):
    first = lax.axis_index("c") == 0
    low = lax.axis_index("h") == 0
    points, width = latents.shape[1], latents.shape[2]
    fields = w_out.shape[1]
    rows = w_mix.shape[0]
    half = width // 2

    def pick(a, b):
        return jnp.where(first, a, b)

    mine = pick(w_mix[:, :half], w_mix[:, half:])
    far = lax.ppermute(mine, ("far", "h"), ACROSS)
    near = jnp.where(low, jnp.concatenate([mine, far], 0), jnp.concatenate([far, mine], 0))
    w_own = all_to_all(copies(near, Y * X), PLANE).reshape(width, half)
    out_own = pick(w_out[:half], w_out[half:])

    lat_own = latents[0]
    lat_oth = lax.ppermute(lat_own, "c", SWAP)
    pre_own = dot(lat_own, w_own, 1, 0)
    hid_own = jax.nn.gelu(pre_own).astype(bf16)
    pre_oth = dot(lat_oth, w_own, 1, 0)
    hid_oth = jax.nn.gelu(pre_oth).astype(bf16)
    fc_own, fc_oth = dot(out_own, hid_own, 0, 1), dot(out_own, hid_oth, 0, 1)

    rest = lax.ppermute(jnp.stack([fc_oth, fc_own]), "c", SWAP)
    fc_own = fc_own + rest[0] + bias[:, None]
    fc_oth = fc_oth + rest[1] + bias[:, None]
    members = all_to_all(copies(fc_own, Z), RING)
    others = lax.ppermute(members, "c", SWAP)
    g_own, terms = pairwise(fc_own, members, others, truth, area)
    g_oth, unused_terms = pairwise(fc_oth, members, others, truth, area)

    like = jax.ShapeDtypeStruct
    gp_own, gp_oth, sent = call(
        backward_kernel,
        [
            like((points, half), bf16),
            like((points, half), bf16),
            like((Y * X, H * rows + 32, half), bf16),
        ],
        [g_own, g_oth, terms, out_own.T, pre_own, pre_oth, hid_own, hid_oth, lat_own, lat_oth],
        flops=4 * points * half * width,
    )
    got = all_to_all(sent, PLANE)

    piece, hpiece = rows // NEAR, fields // NEAR
    block = pltpu.VMEM((H * piece + 16, half), f32)
    sent, gp_oth = call(
        neighbour_kernel,
        [like((NEAR, H * piece + 16, half), bf16), like((points, half), bf16)],
        [got, gp_oth],
        [block],
        through=True,
    )
    got = all_to_all(sent, "near")
    block = pltpu.VMEM((16, half), f32)
    kernel = functools.partial(across_kernel, piece, hpiece)
    got = all_to_all(call(kernel, like((H * FAR, 16, half), bf16), [got], [block]), ("h", "far"))

    kernel = functools.partial(gather_kernel, piece, hpiece)
    sent = call(kernel, like((NEAR * CORES, 16, half), bf16), [got], [block])
    got = all_to_all(sent, ("near", "c"))
    grad_mix, grad_out, grad_bias, loss = call(
        functools.partial(assemble_kernel, points * Y * X * H),
        [
            like((rows, width), f32),
            like((fields, width), f32),
            like((1, fields), f32),
            like((1, 1), f32),
        ],
        [got],
    )

    grad_rows = lax.ppermute(dot(gp_oth, w_own, 1, 1).astype(bf16), "c", SWAP)
    grad_latents = (dot(gp_own, w_own, 1, 1) + grad_rows.astype(f32)).astype(bf16)[None]
    return grad_latents, grad_mix, grad_out.T, grad_bias[0], loss[0, 0]


def solution(mesh):
    shape = (FAR, NEAR, CORES, Y, X, H)
    fine = Mesh(mesh.devices.reshape(shape), ("far", "near", "c", "y", "x", "h"))
    in_specs = (P(ENS, SPACE, None), P(SPACE, None), P(), P(), P(None, SPACE), P(SPACE))
    out_specs = (P(ENS, SPACE, None), P(SPACE, None), P(), P(), P())
    return jax.shard_map(
        body, mesh=fine, in_specs=in_specs, out_specs=out_specs, check_vma=False
    )
```

```python
import functools

import jax
import jax.numpy as jnp
from jax import lax
from jax.experimental import pallas as pl
from jax.experimental.pallas import tpu as pltpu
from jax.sharding import Mesh
from jax.sharding import PartitionSpec as P

M = 16
smoothing = 0.1
FAR, NEAR, CORES, Y, X, H = 2, 4, 2, 4, 4, 2
Z = FAR * NEAR
RING = ("far", "near")
ENS, SPACE, PLANE = ("far", "near", "c"), ("y", "x", "h"), ("y", "x")
f32, bf16 = jnp.float32, jnp.bfloat16
SWAP = ((0, 1), (1, 0))
ACROSS = tuple((far * H + h, (1 - far) * H + 1 - h) for far in range(FAR) for h in range(H))


LANES = 128


def split_row(values, width):
    first = values.astype(bf16).astype(f32)
    second = (values - first).astype(bf16).astype(f32)
    third = values - first - second
    return jnp.concatenate(
        [first, second, third, jnp.zeros((1, width - 3 * LANES), f32)], 1
    )


def joined_row(row):
    return row[:, :LANES] + row[:, LANES : 2 * LANES] + row[:, 2 * LANES : 3 * LANES]


def total(ref):
    result = ref[0].astype(f32)
    for k in range(1, ref.shape[0]):
        result = result + ref[k].astype(f32)
    return result


def call(kernel, shapes, operands, scratch=(), flops=0, through=False):
    vmem = pl.BlockSpec(memory_space=pltpu.VMEM)
    many = isinstance(shapes, list)
    size = sum(o.size * o.dtype.itemsize for o in operands)
    in_specs = [vmem] * len(operands)
    out_specs = [vmem] * len(shapes) if many else vmem
    aliases = {}
    if through:
        in_specs[-1] = out_specs[-1] = pl.BlockSpec(memory_space=pl.ANY)
        aliases = {len(operands) - 1: len(shapes) - 1}
    return pl.pallas_call(
        kernel,
        out_shape=shapes,
        in_specs=in_specs,
        out_specs=out_specs,
        input_output_aliases=aliases,
        scratch_shapes=list(scratch),
        compiler_params=pltpu.CompilerParams(vmem_limit_bytes=40 << 20),
        cost_estimate=pl.CostEstimate(flops=flops, bytes_accessed=size, transcendentals=0),
    )(*operands)


def gelu_slope(x):
    scale = 0.7978845608028654
    square = x * x
    t = jnp.tanh(scale * x * (1.0 + 0.044715 * square))
    return 0.5 * (1.0 + t) + (0.5 * scale) * x * (1.0 - t * t) * (1.0 + 0.134145 * square)


def forecast_kernel(out, hid_own, hid_oth, part):
    fields = out.shape[0]
    part[:fields] = dot(out[...], hid_own[...], 1, 1)
    part[fields:] = dot(out[...], hid_oth[...], 1, 1)


def backward_kernel(
    g_own, g_oth, terms, out, pre_own, pre_oth, hid_own, hid_oth, lat_own, lat_oth,
    gp_own, gp_oth, sent,
):
    peers, rows = sent.shape[0], lat_own.shape[1] // sent.shape[0]
    fields, half = out.shape
    for g, pre, gp in ((g_own, pre_own, gp_own), (g_oth, pre_oth, gp_oth)):
        for k in range(0, pre.shape[0], 128):
            hidden = dot(g[:, k : k + 128], out[...], 0, 0)
            gp[k : k + 128] = (hidden * gelu_slope(pre[k : k + 128])).astype(bf16)
    step = 4
    for k in range(0, peers, step):
        columns = slice(k * rows, (k + step) * rows)
        mix = dot(lat_own[:, columns], gp_own[...], 0, 0)
        mix = mix + dot(lat_oth[:, columns], gp_oth[...], 0, 0)
        sent[k : k + step, :rows] = mix.astype(bf16).reshape(step, rows, half)

    head = dot(g_own[...], hid_own[...], 1, 0) + dot(g_oth[...], hid_oth[...], 1, 0)
    sums = jnp.sum(g_own[...].astype(f32), axis=1, keepdims=True)
    lane = lax.broadcasted_iota(jnp.int32, (fields, LANES), 1)
    field = lax.broadcasted_iota(jnp.int32, (fields, LANES), 0)
    values = jnp.sum(jnp.where(lane == field, sums, 0.0), axis=0, keepdims=True)
    loss = jnp.sum(jnp.sum(terms[...], axis=1, keepdims=True), axis=0, keepdims=True)
    values = jnp.where(lane[:1] == fields, loss, values)
    tail = jnp.where(
        lax.broadcasted_iota(jnp.int32, (16, half), 0) == 0, split_row(values, half), 0.0
    )
    for k in range(peers):
        sent[k, rows : rows + fields] = head.astype(bf16)
        sent[k, rows + fields :] = tail.astype(bf16)


def partial_kernel(gp, weight, rows):
    rows[...] = dot(gp[...], weight[...], 1, 1).astype(bf16)


def latents_kernel(gp, weight, other, rows):
    rows[...] = (dot(gp[...], weight[...], 1, 1) + other[...].astype(f32)).astype(bf16)


def pack(block, mix, head, values):
    start = 0
    for part in (*mix, head, split_row(values, block.shape[1])):
        block[start : start + part.shape[0]] = part
        start += part.shape[0]
    block[start:] = jnp.zeros((block.shape[0] - start, block.shape[1]), f32)
    return block[...].astype(bf16)


def neighbour_kernel(got, unused_in, sent, unused_out, block):
    rows, fields = got.shape[1] - 32, 16
    piece, hpiece = rows // H // NEAR, fields // NEAR
    whole = total(got)
    values = joined_row(whole[rows + fields : rows + fields + 1])
    for n in range(NEAR):
        mix = [
            whole[h * NEAR * piece + n * piece : h * NEAR * piece + (n + 1) * piece]
            for h in range(H)
        ]
        head = whole[rows + n * hpiece : rows + (n + 1) * hpiece]
        sent[n] = pack(block, mix, head, values)


def across_kernel(piece, hpiece, got, sent, block):
    whole = total(got)
    start = H * piece + hpiece
    values = joined_row(whole[start : start + 1])
    for h in range(H):
        mix = whole[h * piece : (h + 1) * piece]
        packed = pack(block, [mix], whole[H * piece : start], values)
        for far in range(FAR):
            sent[h * FAR + far] = packed


def gather_kernel(piece, hpiece, got, sent, block):
    whole = total(got)
    start = piece + hpiece
    values = joined_row(whole[start : start + 1])
    packed = pack(block, [whole[:piece]], whole[piece:start], values)
    for k in range(NEAR * CORES):
        sent[k] = packed


def assemble_kernel(count, got, mix, head, bias, loss):
    half = got.shape[2]
    piece, hpiece = mix.shape[0] // NEAR, head.shape[0] // NEAR
    for n in range(NEAR):
        for c in range(CORES):
            block = got[n * CORES + c].astype(f32)
            columns = slice(c * half, (c + 1) * half)
            mix[n * piece : (n + 1) * piece, columns] = block[:piece]
            head[n * hpiece : (n + 1) * hpiece, columns] = block[piece : piece + hpiece]
            if n == 0:
                row = joined_row(block[piece + hpiece : piece + hpiece + 1])
                values = row if c == 0 else values + row
    fields = head.shape[0]
    bias[...] = values[:, :fields]
    loss[...] = values[:, fields : fields + 1] / count


def member_sums(chosen, members):
    differ = chosen[None] - members
    smooth = jnp.sqrt(differ * differ + smoothing * smoothing)
    return jnp.sum(differ / smooth, axis=0), jnp.sum(smooth, axis=0)


def pairwise(chosen, members, others, observed, weights):
    slope, smooth = member_sums(chosen, members)
    slope_oth, smooth_oth = member_sums(chosen, others)
    slope, smooth = slope + slope_oth, smooth + smooth_oth
    count_all = float(M)
    pairs_norm = count_all * (count_all - 1.0)
    to_truth = chosen - observed
    absolute = jnp.sqrt(to_truth * to_truth + smoothing * smoothing)
    gradient = weights * (to_truth / absolute / count_all - slope / pairs_norm)
    terms = weights * (absolute / count_all - (smooth - smoothing) / (2.0 * pairs_norm))
    return gradient.astype(bf16), terms


def all_to_all(x, axes):
    return lax.all_to_all(x, axes, 0, 0, tiled=True)


def copies(x, count):
    return jnp.broadcast_to(x[None], (count,) + x.shape)


def dot(a, b, ca, cb):
    return lax.dot_general(a, b, (((ca,), (cb,)), ((), ())), preferred_element_type=f32)


def body(latents, w_mix, w_out, bias, truth, area):
    first = lax.axis_index("c") == 0
    low = lax.axis_index("h") == 0
    points, width = latents.shape[1], latents.shape[2]
    fields = w_out.shape[1]
    rows = w_mix.shape[0]
    half = width // 2

    def pick(a, b):
        return jnp.where(first, a, b)

    mine = pick(w_mix[:, :half], w_mix[:, half:])
    far = lax.ppermute(mine, ("far", "h"), ACROSS)
    near = jnp.where(low, jnp.concatenate([mine, far], 0), jnp.concatenate([far, mine], 0))
    w_own = all_to_all(copies(near, Y * X), PLANE).reshape(width, half)
    out_own = pick(w_out.T[:, :half], w_out.T[:, half:])

    lat_own = latents[0]
    lat_oth = lax.ppermute(lat_own, "c", SWAP)
    pre_own = dot(lat_own, w_own, 1, 0)
    hid_own = jax.nn.gelu(pre_own).astype(bf16)
    pre_oth = dot(lat_oth, w_own, 1, 0)
    hid_oth = jax.nn.gelu(pre_oth).astype(bf16)

    like = jax.ShapeDtypeStruct
    part = call(
        forecast_kernel,
        like((2 * fields, points), f32),
        [out_own, hid_own, hid_oth],
        flops=4 * fields * points * half,
    )
    both = lax.all_gather(part, "c", axis=0)
    rest = pick(both[1], both[0])
    fc_own = part[:fields] + rest[fields:] + bias[:, None]
    fc_oth = part[fields:] + rest[:fields] + bias[:, None]
    members = all_to_all(copies(fc_own, Z), RING)
    both = lax.all_gather(members, "c", axis=0)
    others = pick(both[1], both[0])
    g_own, terms = pairwise(fc_own, members, others, truth, area)
    g_oth, unused_terms = pairwise(fc_oth, members, others, truth, area)

    gp_own, gp_oth, sent = call(
        backward_kernel,
        [
            like((points, half), bf16),
            like((points, half), bf16),
            like((Y * X, H * rows + 32, half), bf16),
        ],
        [g_own, g_oth, terms, out_own, pre_own, pre_oth, hid_own, hid_oth, lat_own, lat_oth],
        flops=4 * points * half * width,
    )
    got = all_to_all(sent, PLANE)

    piece, hpiece = rows // NEAR, fields // NEAR
    block = pltpu.VMEM((H * piece + 16, half), f32)
    sent, gp_oth = call(
        neighbour_kernel,
        [like((NEAR, H * piece + 16, half), bf16), like((points, half), bf16)],
        [got, gp_oth],
        [block],
        through=True,
    )
    got = all_to_all(sent, "near")
    block = pltpu.VMEM((16, half), f32)
    kernel = functools.partial(across_kernel, piece, hpiece)
    got = all_to_all(call(kernel, like((H * FAR, 16, half), bf16), [got], [block]), ("h", "far"))

    kernel = functools.partial(gather_kernel, piece, hpiece)
    sent = call(kernel, like((NEAR * CORES, 16, half), bf16), [got], [block])
    got = all_to_all(sent, ("near", "c"))
    grad_mix, grad_out, grad_bias, loss = call(
        functools.partial(assemble_kernel, points * Y * X * H),
        [
            like((rows, width), f32),
            like((fields, width), f32),
            like((1, fields), f32),
            like((1, 1), f32),
        ],
        [got],
    )

    rows_like, work = like((points, width), bf16), 16 * points * half * width
    grad_rows = call(partial_kernel, rows_like, [gp_oth, w_own], flops=work)
    grad_rows = lax.ppermute(grad_rows, "c", SWAP)
    grad_latents = call(latents_kernel, rows_like, [gp_own, w_own, grad_rows], flops=work)[None]
    return grad_latents, grad_mix, grad_out.T, grad_bias[0], loss[0, 0]


def solution(mesh):
    shape = (FAR, NEAR, CORES, Y, X, H)
    fine = Mesh(mesh.devices.reshape(shape), ("far", "near", "c", "y", "x", "h"))
    in_specs = (P(ENS, SPACE, None), P(SPACE, None), P(), P(), P(None, SPACE), P(SPACE))
    out_specs = (P(ENS, SPACE, None), P(SPACE, None), P(), P(), P())
    return jax.shard_map(
        body, mesh=fine, in_specs=in_specs, out_specs=out_specs, check_vma=False
    )
```

```python
import functools

import jax
import jax.numpy as jnp
from jax import lax
from jax.experimental import pallas as pl
from jax.experimental.pallas import tpu as pltpu
from jax.sharding import Mesh
from jax.sharding import PartitionSpec as P

M = 16
smoothing = 0.1
FAR, NEAR, CORES, Y, X, H = 2, 4, 2, 4, 4, 2
Z = FAR * NEAR
RING = ("far", "near")
ENS, SPACE, PLANE = ("far", "near", "c"), ("y", "x", "h"), ("y", "x")
f32, bf16 = jnp.float32, jnp.bfloat16
SWAP = ((0, 1), (1, 0))
ACROSS = tuple((far * H + h, (1 - far) * H + 1 - h) for far in range(FAR) for h in range(H))


LANES = 128


def split_row(values, width):
    first = values.astype(bf16).astype(f32)
    second = (values - first).astype(bf16).astype(f32)
    third = values - first - second
    return jnp.concatenate(
        [first, second, third, jnp.zeros((1, width - 3 * LANES), f32)], 1
    )


def joined_row(row):
    return row[:, :LANES] + row[:, LANES : 2 * LANES] + row[:, 2 * LANES : 3 * LANES]


def total(ref):
    result = ref[0].astype(f32)
    for k in range(1, ref.shape[0]):
        result = result + ref[k].astype(f32)
    return result


def call(kernel, shapes, operands, scratch=(), flops=0, through=0):
    vmem = pl.BlockSpec(memory_space=pltpu.VMEM)
    many = isinstance(shapes, list)
    size = sum(o.size * o.dtype.itemsize for o in operands)
    in_specs = [vmem] * len(operands)
    out_specs = [vmem] * len(shapes) if many else vmem
    aliases = {}
    for k in range(1, through + 1):
        in_specs[-k] = out_specs[-k] = pl.BlockSpec(memory_space=pl.ANY)
        aliases[len(operands) - k] = len(shapes) - k
    return pl.pallas_call(
        kernel,
        out_shape=shapes,
        in_specs=in_specs,
        out_specs=out_specs,
        input_output_aliases=aliases,
        scratch_shapes=list(scratch),
        compiler_params=pltpu.CompilerParams(vmem_limit_bytes=40 << 20),
        cost_estimate=pl.CostEstimate(flops=flops, bytes_accessed=size, transcendentals=0),
    )(*operands)


def gelu_slope(x):
    scale = 0.7978845608028654
    square = x * x
    t = jnp.tanh(scale * x * (1.0 + 0.044715 * square))
    return 0.5 * (1.0 + t) + (0.5 * scale) * x * (1.0 - t * t) * (1.0 + 0.134145 * square)


def forecast_kernel(out, hid_own, hid_oth, part):
    fields = out.shape[0]
    part[:fields] = dot(out[...], hid_own[...], 1, 1)
    part[fields:] = dot(out[...], hid_oth[...], 1, 1)


def backward_kernel(
    g_own, g_oth, terms, out, pre_own, pre_oth, hid_own, hid_oth, lat_own, lat_oth,
    gp_own, gp_oth, sent,
):
    peers, rows = sent.shape[0], lat_own.shape[1] // sent.shape[0]
    fields, half = out.shape
    for g, pre, gp in ((g_own, pre_own, gp_own), (g_oth, pre_oth, gp_oth)):
        for k in range(0, pre.shape[0], 128):
            hidden = dot(g[:, k : k + 128], out[...], 0, 0)
            gp[k : k + 128] = (hidden * gelu_slope(pre[k : k + 128])).astype(bf16)
    step = 4
    for k in range(0, peers, step):
        columns = slice(k * rows, (k + step) * rows)
        mix = dot(lat_own[:, columns], gp_own[...], 0, 0)
        mix = mix + dot(lat_oth[:, columns], gp_oth[...], 0, 0)
        sent[k : k + step, :rows] = mix.astype(bf16).reshape(step, rows, half)

    head = dot(g_own[...], hid_own[...], 1, 0) + dot(g_oth[...], hid_oth[...], 1, 0)
    sums = jnp.sum(g_own[...].astype(f32), axis=1, keepdims=True)
    lane = lax.broadcasted_iota(jnp.int32, (fields, LANES), 1)
    field = lax.broadcasted_iota(jnp.int32, (fields, LANES), 0)
    values = jnp.sum(jnp.where(lane == field, sums, 0.0), axis=0, keepdims=True)
    loss = jnp.sum(jnp.sum(terms[...], axis=1, keepdims=True), axis=0, keepdims=True)
    values = jnp.where(lane[:1] == fields, loss, values)
    tail = jnp.where(
        lax.broadcasted_iota(jnp.int32, (16, half), 0) == 0, split_row(values, half), 0.0
    )
    for k in range(peers):
        sent[k, rows : rows + fields] = head.astype(bf16)
        sent[k, rows + fields :] = tail.astype(bf16)


def partial_kernel(gp, weight, rows):
    rows[...] = dot(gp[...], weight[...], 1, 1).astype(bf16)


def latents_kernel(gp, weight, other, rows):
    rows[...] = (dot(gp[...], weight[...], 1, 1) + other[...].astype(f32)).astype(bf16)


def pack(block, mix, head, values):
    start = 0
    for part in (*mix, head, split_row(values, block.shape[1])):
        block[start : start + part.shape[0]] = part
        start += part.shape[0]
    block[start:] = jnp.zeros((block.shape[0] - start, block.shape[1]), f32)
    return block[...].astype(bf16)


def neighbour_kernel(got, unused_a, unused_b, sent, unused_c, unused_d, block):
    rows, fields = got.shape[1] - 32, 16
    piece, hpiece = rows // H // NEAR, fields // NEAR
    whole = total(got)
    values = joined_row(whole[rows + fields : rows + fields + 1])
    for n in range(NEAR):
        mix = [
            whole[h * NEAR * piece + n * piece : h * NEAR * piece + (n + 1) * piece]
            for h in range(H)
        ]
        head = whole[rows + n * hpiece : rows + (n + 1) * hpiece]
        sent[n] = pack(block, mix, head, values)


def across_kernel(piece, hpiece, got, sent, block):
    whole = total(got)
    start = H * piece + hpiece
    values = joined_row(whole[start : start + 1])
    for h in range(H):
        mix = whole[h * piece : (h + 1) * piece]
        packed = pack(block, [mix], whole[H * piece : start], values)
        for far in range(FAR):
            sent[h * FAR + far] = packed


def gather_kernel(piece, hpiece, got, sent, block):
    whole = total(got)
    start = piece + hpiece
    values = joined_row(whole[start : start + 1])
    packed = pack(block, [whole[:piece]], whole[piece:start], values)
    for k in range(NEAR * CORES):
        sent[k] = packed


def assemble_kernel(count, got, mix, head, bias, loss):
    half = got.shape[2]
    piece, hpiece = mix.shape[0] // NEAR, head.shape[0] // NEAR
    for n in range(NEAR):
        for c in range(CORES):
            block = got[n * CORES + c].astype(f32)
            columns = slice(c * half, (c + 1) * half)
            mix[n * piece : (n + 1) * piece, columns] = block[:piece]
            head[n * hpiece : (n + 1) * hpiece, columns] = block[piece : piece + hpiece]
            if n == 0:
                row = joined_row(block[piece + hpiece : piece + hpiece + 1])
                values = row if c == 0 else values + row
    fields = head.shape[0]
    bias[...] = values[:, :fields]
    loss[...] = values[:, fields : fields + 1] / count


def member_sums(chosen, members):
    differ = chosen[None] - members
    smooth = jnp.sqrt(differ * differ + smoothing * smoothing)
    return jnp.sum(differ / smooth, axis=0), jnp.sum(smooth, axis=0)


def pairwise(chosen, members, others, observed, weights):
    slope, smooth = member_sums(chosen, members)
    slope_oth, smooth_oth = member_sums(chosen, others)
    slope, smooth = slope + slope_oth, smooth + smooth_oth
    count_all = float(M)
    pairs_norm = count_all * (count_all - 1.0)
    to_truth = chosen - observed
    absolute = jnp.sqrt(to_truth * to_truth + smoothing * smoothing)
    gradient = weights * (to_truth / absolute / count_all - slope / pairs_norm)
    terms = weights * (absolute / count_all - (smooth - smoothing) / (2.0 * pairs_norm))
    return gradient.astype(bf16), terms


def all_to_all(x, axes):
    return lax.all_to_all(x, axes, 0, 0, tiled=True)


def copies(x, count):
    return jnp.broadcast_to(x[None], (count,) + x.shape)


def dot(a, b, ca, cb):
    return lax.dot_general(a, b, (((ca,), (cb,)), ((), ())), preferred_element_type=f32)


def body(latents, w_mix, w_out, bias, truth, area):
    first = lax.axis_index("c") == 0
    low = lax.axis_index("h") == 0
    points, width = latents.shape[1], latents.shape[2]
    fields = w_out.shape[1]
    rows = w_mix.shape[0]
    half = width // 2

    def pick(a, b):
        return jnp.where(first, a, b)

    mine = pick(w_mix[:, :half], w_mix[:, half:])
    far = lax.ppermute(mine, ("far", "h"), ACROSS)
    near = jnp.where(low, jnp.concatenate([mine, far], 0), jnp.concatenate([far, mine], 0))
    w_own = all_to_all(copies(near, Y * X), PLANE).reshape(width, half)
    out_own = pick(w_out.T[:, :half], w_out.T[:, half:])

    lat_own = latents[0]
    lat_oth = lax.ppermute(lat_own, "c", SWAP)
    pre_own = dot(lat_own, w_own, 1, 0)
    hid_own = jax.nn.gelu(pre_own).astype(bf16)
    pre_oth = dot(lat_oth, w_own, 1, 0)
    hid_oth = jax.nn.gelu(pre_oth).astype(bf16)

    like = jax.ShapeDtypeStruct
    part = call(
        forecast_kernel,
        like((2 * fields, points), f32),
        [out_own, hid_own, hid_oth],
        flops=4 * fields * points * half,
    )
    both = lax.all_gather(part, "c", axis=0)
    rest = pick(both[1], both[0])
    fc_own = part[:fields] + rest[fields:] + bias[:, None]
    fc_oth = part[fields:] + rest[:fields] + bias[:, None]
    members = all_to_all(copies(fc_own, Z), RING)
    both = lax.all_gather(members, "c", axis=0)
    others = pick(both[1], both[0])
    g_own, terms = pairwise(fc_own, members, others, truth, area)
    g_oth, unused_terms = pairwise(fc_oth, members, others, truth, area)

    gp_own, gp_oth, sent = call(
        backward_kernel,
        [
            like((points, half), bf16),
            like((points, half), bf16),
            like((Y * X, H * rows + 32, half), bf16),
        ],
        [g_own, g_oth, terms, out_own, pre_own, pre_oth, hid_own, hid_oth, lat_own, lat_oth],
        flops=4 * points * half * width,
    )
    got = all_to_all(sent, PLANE)

    piece, hpiece = rows // NEAR, fields // NEAR
    block = pltpu.VMEM((H * piece + 16, half), f32)
    gp_like = like((points, half), bf16)
    sent, gp_own, gp_oth = call(
        neighbour_kernel,
        [like((NEAR, H * piece + 16, half), bf16), gp_like, gp_like],
        [got, gp_own, gp_oth],
        [block],
        through=2,
    )
    got = all_to_all(sent, "near")
    block = pltpu.VMEM((16, half), f32)
    kernel = functools.partial(across_kernel, piece, hpiece)
    got = all_to_all(call(kernel, like((H * FAR, 16, half), bf16), [got], [block]), ("h", "far"))

    kernel = functools.partial(gather_kernel, piece, hpiece)
    sent = call(kernel, like((NEAR * CORES, 16, half), bf16), [got], [block])
    got = all_to_all(sent, ("near", "c"))
    grad_mix, grad_out, grad_bias, loss = call(
        functools.partial(assemble_kernel, points * Y * X * H),
        [
            like((rows, width), f32),
            like((fields, width), f32),
            like((1, fields), f32),
            like((1, 1), f32),
        ],
        [got],
    )

    rows_like, work = like((points, width), bf16), 16 * points * half * width
    grad_rows = call(partial_kernel, rows_like, [gp_oth, w_own], flops=work)
    grad_rows = lax.ppermute(grad_rows, "c", SWAP)
    grad_latents = call(latents_kernel, rows_like, [gp_own, w_own, grad_rows], flops=work)[None]
    return grad_latents, grad_mix, grad_out.T, grad_bias[0], loss[0, 0]


def solution(mesh):
    shape = (FAR, NEAR, CORES, Y, X, H)
    fine = Mesh(mesh.devices.reshape(shape), ("far", "near", "c", "y", "x", "h"))
    in_specs = (P(ENS, SPACE, None), P(SPACE, None), P(), P(), P(None, SPACE), P(SPACE))
    out_specs = (P(ENS, SPACE, None), P(SPACE, None), P(), P(), P())
    return jax.shard_map(
        body, mesh=fine, in_specs=in_specs, out_specs=out_specs, check_vma=False
    )
```

```python
import functools

import jax
import jax.numpy as jnp
from jax import lax
from jax.experimental import pallas as pl
from jax.experimental.pallas import tpu as pltpu
from jax.sharding import Mesh
from jax.sharding import PartitionSpec as P

M = 16
smoothing = 0.1
FAR, NEAR, CORES, Y, X, H = 2, 4, 2, 4, 4, 2
Z = FAR * NEAR
RING = ("far", "near")
ENS, SPACE, PLANE = ("far", "near", "c"), ("y", "x", "h"), ("y", "x")
f32, bf16 = jnp.float32, jnp.bfloat16
SWAP = ((0, 1), (1, 0))
ACROSS = tuple((far * H + h, (1 - far) * H + 1 - h) for far in range(FAR) for h in range(H))


LANES = 128


def split_row(values, width):
    first = values.astype(bf16).astype(f32)
    second = (values - first).astype(bf16).astype(f32)
    third = values - first - second
    return jnp.concatenate(
        [first, second, third, jnp.zeros((1, width - 3 * LANES), f32)], 1
    )


def joined_row(row):
    return row[:, :LANES] + row[:, LANES : 2 * LANES] + row[:, 2 * LANES : 3 * LANES]


def total(ref):
    result = ref[0].astype(f32)
    for k in range(1, ref.shape[0]):
        result = result + ref[k].astype(f32)
    return result


def call(kernel, shapes, operands, scratch=(), flops=0, through=0):
    vmem = pl.BlockSpec(memory_space=pltpu.VMEM)
    many = isinstance(shapes, list)
    size = sum(o.size * o.dtype.itemsize for o in operands)
    in_specs = [vmem] * len(operands)
    out_specs = [vmem] * len(shapes) if many else vmem
    aliases = {}
    for k in range(1, through + 1):
        in_specs[-k] = out_specs[-k] = pl.BlockSpec(memory_space=pl.ANY)
        aliases[len(operands) - k] = len(shapes) - k
    return pl.pallas_call(
        kernel,
        out_shape=shapes,
        in_specs=in_specs,
        out_specs=out_specs,
        input_output_aliases=aliases,
        scratch_shapes=list(scratch),
        compiler_params=pltpu.CompilerParams(vmem_limit_bytes=40 << 20),
        cost_estimate=pl.CostEstimate(flops=flops, bytes_accessed=size, transcendentals=0),
    )(*operands)


def gelu_slope(x):
    scale = 0.7978845608028654
    square = x * x
    t = jnp.tanh(scale * x * (1.0 + 0.044715 * square))
    return 0.5 * (1.0 + t) + (0.5 * scale) * x * (1.0 - t * t) * (1.0 + 0.134145 * square)


def forecast_kernel(out, hid_own, hid_oth, part):
    fields = out.shape[0]
    part[:fields] = dot(out[...], hid_own[...], 1, 1)
    part[fields:] = dot(out[...], hid_oth[...], 1, 1)


def backward_kernel(
    g_own, g_oth, terms, out, pre_own, pre_oth, hid_own, hid_oth, lat_own, lat_oth,
    gp_own, gp_oth, sent,
):
    peers, rows = sent.shape[0], lat_own.shape[1] // sent.shape[0]
    fields, half = out.shape
    for g, pre, gp in ((g_own, pre_own, gp_own), (g_oth, pre_oth, gp_oth)):
        for k in range(0, pre.shape[0], 128):
            hidden = dot(g[:, k : k + 128], out[...], 0, 0)
            gp[k : k + 128] = (hidden * gelu_slope(pre[k : k + 128])).astype(bf16)
    head = dot(g_own[...], hid_own[...], 1, 0) + dot(g_oth[...], hid_oth[...], 1, 0)
    sums = jnp.sum(g_own[...].astype(f32), axis=1, keepdims=True)
    lane = lax.broadcasted_iota(jnp.int32, (fields, LANES), 1)
    field = lax.broadcasted_iota(jnp.int32, (fields, LANES), 0)
    values = jnp.sum(jnp.where(lane == field, sums, 0.0), axis=0, keepdims=True)
    loss = jnp.sum(jnp.sum(terms[...], axis=1, keepdims=True), axis=0, keepdims=True)
    values = jnp.where(lane[:1] == fields, loss, values)
    tail = jnp.where(
        lax.broadcasted_iota(jnp.int32, (8, half), 0) == 0, split_row(values, half), 0.0
    )
    step = 4
    for k in range(0, peers, step):
        columns = slice(k * rows, (k + step) * rows)
        mix = dot(lat_own[:, columns], gp_own[...], 0, 0)
        mix = mix + dot(lat_oth[:, columns], gp_oth[...], 0, 0)
        for j in range(step):
            block = [mix[j * rows : (j + 1) * rows], head, tail]
            sent[k + j] = jnp.concatenate(block, 0).astype(bf16)


def partial_kernel(gp, weight, rows):
    rows[...] = dot(gp[...], weight[...], 1, 1).astype(bf16)


def latents_kernel(gp, weight, other, rows):
    rows[...] = (dot(gp[...], weight[...], 1, 1) + other[...].astype(f32)).astype(bf16)


def pack(block, mix, head, values):
    start = 0
    for part in (*mix, head, split_row(values, block.shape[1])):
        block[start : start + part.shape[0]] = part
        start += part.shape[0]
    block[start:] = jnp.zeros((block.shape[0] - start, block.shape[1]), f32)
    return block[...].astype(bf16)


def neighbour_kernel(got, unused_a, unused_b, sent, unused_c, unused_d, block):
    rows, fields = got.shape[1] - 24, 16
    piece, hpiece = rows // H // NEAR, fields // NEAR
    whole = total(got)
    values = joined_row(whole[rows + fields : rows + fields + 1])
    for n in range(NEAR):
        mix = [
            whole[h * NEAR * piece + n * piece : h * NEAR * piece + (n + 1) * piece]
            for h in range(H)
        ]
        head = whole[rows + n * hpiece : rows + (n + 1) * hpiece]
        sent[n] = pack(block, mix, head, values)


def across_kernel(piece, hpiece, got, sent, block):
    whole = total(got)
    start = H * piece + hpiece
    values = joined_row(whole[start : start + 1])
    for h in range(H):
        mix = whole[h * piece : (h + 1) * piece]
        packed = pack(block, [mix], whole[H * piece : start], values)
        for far in range(FAR):
            sent[h * FAR + far] = packed


def gather_kernel(piece, hpiece, got, sent, block):
    whole = total(got)
    start = piece + hpiece
    values = joined_row(whole[start : start + 1])
    packed = pack(block, [whole[:piece]], whole[piece:start], values)
    for k in range(NEAR * CORES):
        sent[k] = packed


def assemble_kernel(count, got, mix, head, bias, loss):
    half = got.shape[2]
    piece, hpiece = mix.shape[0] // NEAR, head.shape[0] // NEAR
    for n in range(NEAR):
        for c in range(CORES):
            block = got[n * CORES + c].astype(f32)
            columns = slice(c * half, (c + 1) * half)
            mix[n * piece : (n + 1) * piece, columns] = block[:piece]
            head[n * hpiece : (n + 1) * hpiece, columns] = block[piece : piece + hpiece]
            if n == 0:
                row = joined_row(block[piece + hpiece : piece + hpiece + 1])
                values = row if c == 0 else values + row
    fields = head.shape[0]
    bias[...] = values[:, :fields]
    loss[...] = values[:, fields : fields + 1] / count


def member_sums(chosen, members):
    differ = chosen[None] - members
    smooth = jnp.sqrt(differ * differ + smoothing * smoothing)
    return jnp.sum(differ / smooth, axis=0), jnp.sum(smooth, axis=0)


def pairwise(chosen, members, others, observed, weights):
    slope, smooth = member_sums(chosen, members)
    slope_oth, smooth_oth = member_sums(chosen, others)
    slope, smooth = slope + slope_oth, smooth + smooth_oth
    count_all = float(M)
    pairs_norm = count_all * (count_all - 1.0)
    to_truth = chosen - observed
    absolute = jnp.sqrt(to_truth * to_truth + smoothing * smoothing)
    gradient = weights * (to_truth / absolute / count_all - slope / pairs_norm)
    terms = weights * (absolute / count_all - (smooth - smoothing) / (2.0 * pairs_norm))
    return gradient.astype(bf16), terms


def all_to_all(x, axes):
    return lax.all_to_all(x, axes, 0, 0, tiled=True)


def copies(x, count):
    return jnp.broadcast_to(x[None], (count,) + x.shape)


def dot(a, b, ca, cb):
    return lax.dot_general(a, b, (((ca,), (cb,)), ((), ())), preferred_element_type=f32)


def body(latents, w_mix, w_out, bias, truth, area):
    first = lax.axis_index("c") == 0
    low = lax.axis_index("h") == 0
    points, width = latents.shape[1], latents.shape[2]
    fields = w_out.shape[1]
    rows = w_mix.shape[0]
    half = width // 2

    def pick(a, b):
        return jnp.where(first, a, b)

    mine = pick(w_mix[:, :half], w_mix[:, half:])
    far = lax.ppermute(mine, ("far", "h"), ACROSS)
    near = jnp.where(low, jnp.concatenate([mine, far], 0), jnp.concatenate([far, mine], 0))
    w_own = all_to_all(copies(near, Y * X), PLANE).reshape(width, half)
    out_own = pick(w_out.T[:, :half], w_out.T[:, half:])

    lat_own = latents[0]
    lat_oth = lax.ppermute(lat_own, "c", SWAP)
    pre_own = dot(lat_own, w_own, 1, 0)
    hid_own = jax.nn.gelu(pre_own).astype(bf16)
    pre_oth = dot(lat_oth, w_own, 1, 0)
    hid_oth = jax.nn.gelu(pre_oth).astype(bf16)

    like = jax.ShapeDtypeStruct
    part = call(
        forecast_kernel,
        like((2 * fields, points), f32),
        [out_own, hid_own, hid_oth],
        flops=4 * fields * points * half,
    )
    both = lax.all_gather(part, "c", axis=0)
    rest = pick(both[1], both[0])
    fc_own = part[:fields] + rest[fields:] + bias[:, None]
    fc_oth = part[fields:] + rest[:fields] + bias[:, None]
    members = all_to_all(copies(fc_own, Z), RING)
    both = lax.all_gather(members, "c", axis=0)
    others = pick(both[1], both[0])
    g_own, terms = pairwise(fc_own, members, others, truth, area)
    g_oth, unused_terms = pairwise(fc_oth, members, others, truth, area)

    gp_own, gp_oth, sent = call(
        backward_kernel,
        [
            like((points, half), bf16),
            like((points, half), bf16),
            like((Y * X, H * rows + 24, half), bf16),
        ],
        [g_own, g_oth, terms, out_own, pre_own, pre_oth, hid_own, hid_oth, lat_own, lat_oth],
        flops=4 * points * half * width,
    )
    got = all_to_all(sent, PLANE)

    piece, hpiece = rows // NEAR, fields // NEAR
    block = pltpu.VMEM((H * piece + 16, half), f32)
    gp_like = like((points, half), bf16)
    sent, gp_own, gp_oth = call(
        neighbour_kernel,
        [like((NEAR, H * piece + 16, half), bf16), gp_like, gp_like],
        [got, gp_own, gp_oth],
        [block],
        through=2,
    )
    got = all_to_all(sent, "near")
    block = pltpu.VMEM((16, half), f32)
    kernel = functools.partial(across_kernel, piece, hpiece)
    got = all_to_all(call(kernel, like((H * FAR, 16, half), bf16), [got], [block]), ("h", "far"))

    kernel = functools.partial(gather_kernel, piece, hpiece)
    sent = call(kernel, like((NEAR * CORES, 16, half), bf16), [got], [block])
    got = all_to_all(sent, ("near", "c"))
    grad_mix, grad_out, grad_bias, loss = call(
        functools.partial(assemble_kernel, points * Y * X * H),
        [
            like((rows, width), f32),
            like((fields, width), f32),
            like((1, fields), f32),
            like((1, 1), f32),
        ],
        [got],
    )

    rows_like, work = like((points, width), bf16), 16 * points * half * width
    grad_rows = call(partial_kernel, rows_like, [gp_oth, w_own], flops=work)
    grad_rows = lax.ppermute(grad_rows, "c", SWAP)
    grad_latents = call(latents_kernel, rows_like, [gp_own, w_own, grad_rows], flops=work)[None]
    return grad_latents, grad_mix, grad_out.T, grad_bias[0], loss[0, 0]


def solution(mesh):
    shape = (FAR, NEAR, CORES, Y, X, H)
    fine = Mesh(mesh.devices.reshape(shape), ("far", "near", "c", "y", "x", "h"))
    in_specs = (P(ENS, SPACE, None), P(SPACE, None), P(), P(), P(None, SPACE), P(SPACE))
    out_specs = (P(ENS, SPACE, None), P(SPACE, None), P(), P(), P())
    return jax.shard_map(
        body, mesh=fine, in_specs=in_specs, out_specs=out_specs, check_vma=False
    )
```

```python
import functools

import jax
import jax.numpy as jnp
from jax import lax
from jax.experimental import pallas as pl
from jax.experimental.pallas import tpu as pltpu
from jax.sharding import Mesh
from jax.sharding import PartitionSpec as P

M = 16
smoothing = 0.1
FAR, NEAR, CORES, Y, X, H = 2, 4, 2, 4, 4, 2
Z = FAR * NEAR
RING = ("far", "near")
ENS, SPACE, PLANE = ("far", "near", "c"), ("y", "x", "h"), ("y", "x")
f32, bf16 = jnp.float32, jnp.bfloat16
SWAP = ((0, 1), (1, 0))
ACROSS = tuple((far * H + h, (1 - far) * H + 1 - h) for far in range(FAR) for h in range(H))


LANES = 128


def split_row(values, width):
    first = values.astype(bf16).astype(f32)
    second = (values - first).astype(bf16).astype(f32)
    third = values - first - second
    return jnp.concatenate(
        [first, second, third, jnp.zeros((1, width - 3 * LANES), f32)], 1
    )


def joined_row(row):
    return row[:, :LANES] + row[:, LANES : 2 * LANES] + row[:, 2 * LANES : 3 * LANES]


def total(ref):
    result = ref[0].astype(f32)
    for k in range(1, ref.shape[0]):
        result = result + ref[k].astype(f32)
    return result


def call(kernel, shapes, operands, scratch=(), flops=0, through=0):
    vmem = pl.BlockSpec(memory_space=pltpu.VMEM)
    many = isinstance(shapes, list)
    size = sum(o.size * o.dtype.itemsize for o in operands)
    in_specs = [vmem] * len(operands)
    out_specs = [vmem] * len(shapes) if many else vmem
    aliases = {}
    for k in range(1, through + 1):
        in_specs[-k] = out_specs[-k] = pl.BlockSpec(memory_space=pl.ANY)
        aliases[len(operands) - k] = len(shapes) - k
    return pl.pallas_call(
        kernel,
        out_shape=shapes,
        in_specs=in_specs,
        out_specs=out_specs,
        input_output_aliases=aliases,
        scratch_shapes=list(scratch),
        compiler_params=pltpu.CompilerParams(vmem_limit_bytes=40 << 20),
        cost_estimate=pl.CostEstimate(flops=flops, bytes_accessed=size, transcendentals=0),
    )(*operands)


def gelu_slope(x):
    scale = 0.7978845608028654
    square = x * x
    t = jnp.tanh(scale * x * (1.0 + 0.044715 * square))
    return 0.5 * (1.0 + t) + (0.5 * scale) * x * (1.0 - t * t) * (1.0 + 0.134145 * square)


def forecast_kernel(out, hid_own, hid_oth, part):
    fields = out.shape[0]
    part[:fields] = dot(out[...], hid_own[...], 1, 1)
    part[fields:] = dot(out[...], hid_oth[...], 1, 1)


def backward_kernel(
    g_own, g_oth, terms, out, pre_own, pre_oth, hid_own, hid_oth, lat_own, lat_oth,
    gp_own, gp_oth, sent,
):
    peers, rows = sent.shape[0], lat_own.shape[1] // sent.shape[0]
    fields, half = out.shape
    for g, pre, gp in ((g_own, pre_own, gp_own), (g_oth, pre_oth, gp_oth)):
        for k in range(0, pre.shape[0], 128):
            hidden = dot(g[:, k : k + 128], out[...], 0, 0)
            gp[k : k + 128] = (hidden * gelu_slope(pre[k : k + 128])).astype(bf16)
    head = dot(g_own[...], hid_own[...], 1, 0) + dot(g_oth[...], hid_oth[...], 1, 0)
    sums = jnp.sum(g_own[...].astype(f32), axis=1, keepdims=True)
    lane = lax.broadcasted_iota(jnp.int32, (fields, LANES), 1)
    field = lax.broadcasted_iota(jnp.int32, (fields, LANES), 0)
    values = jnp.sum(jnp.where(lane == field, sums, 0.0), axis=0, keepdims=True)
    loss = jnp.sum(jnp.sum(terms[...], axis=1, keepdims=True), axis=0, keepdims=True)
    values = jnp.where(lane[:1] == fields, loss, values)
    tail = jnp.where(
        lax.broadcasted_iota(jnp.int32, (8, half), 0) == 0, split_row(values, half), 0.0
    )
    step = 4
    for k in range(0, peers, step):
        columns = slice(k * rows, (k + step) * rows)
        mix = dot(lat_own[:, columns], gp_own[...], 0, 0)
        mix = mix + dot(lat_oth[:, columns], gp_oth[...], 0, 0)
        for j in range(step):
            block = [mix[j * rows : (j + 1) * rows], head, tail]
            sent[k + j] = jnp.concatenate(block, 0).astype(bf16)


def partial_kernel(gp, weight, rows):
    rows[...] = dot(gp[...], weight[...], 1, 1).astype(bf16)


def latents_kernel(gp, weight, other, rows):
    rows[...] = (dot(gp[...], weight[...], 1, 1) + other[...].astype(f32)).astype(bf16)


def pack(block, mix, head, values):
    start = 0
    for part in (*mix, head, split_row(values, block.shape[1])):
        block[start : start + part.shape[0]] = part
        start += part.shape[0]
    block[start:] = jnp.zeros((block.shape[0] - start, block.shape[1]), f32)
    return block[...].astype(bf16)


def neighbour_kernel(got, unused_a, unused_b, sent, unused_c, unused_d, block):
    rows, fields = got.shape[1] - 24, 16
    piece, hpiece = rows // H // NEAR, fields // NEAR
    whole = total(got)
    values = joined_row(whole[rows + fields : rows + fields + 1])
    for n in range(NEAR):
        mix = [
            whole[h * NEAR * piece + n * piece : h * NEAR * piece + (n + 1) * piece]
            for h in range(H)
        ]
        head = whole[rows + n * hpiece : rows + (n + 1) * hpiece]
        sent[n] = pack(block, mix, head, values)


def across_kernel(piece, hpiece, got, sent, block):
    whole = total(got)
    start = H * piece + hpiece
    values = joined_row(whole[start : start + 1])
    for h in range(H):
        mix = whole[h * piece : (h + 1) * piece]
        packed = pack(block, [mix], whole[H * piece : start], values)
        for far in range(FAR):
            sent[h * FAR + far] = packed


def gather_kernel(piece, hpiece, got, sent, block):
    whole = total(got)
    start = piece + hpiece
    values = joined_row(whole[start : start + 1])
    packed = pack(block, [whole[:piece]], whole[piece:start], values)
    for k in range(NEAR * CORES):
        sent[k] = packed


def assemble_kernel(count, got, unused_in, mix, head, bias, loss, unused_out):
    half = got.shape[2]
    piece, hpiece = mix.shape[0] // NEAR, head.shape[0] // NEAR
    for n in range(NEAR):
        for c in range(CORES):
            block = got[n * CORES + c].astype(f32)
            columns = slice(c * half, (c + 1) * half)
            mix[n * piece : (n + 1) * piece, columns] = block[:piece]
            head[n * hpiece : (n + 1) * hpiece, columns] = block[piece : piece + hpiece]
            if n == 0:
                row = joined_row(block[piece + hpiece : piece + hpiece + 1])
                values = row if c == 0 else values + row
    fields = head.shape[0]
    bias[...] = values[:, :fields]
    loss[...] = values[:, fields : fields + 1] / count


def member_sums(chosen, members):
    differ = chosen[None] - members
    smooth = jnp.sqrt(differ * differ + smoothing * smoothing)
    return jnp.sum(differ / smooth, axis=0), jnp.sum(smooth, axis=0)


def pairwise(chosen, members, others, observed, weights):
    slope, smooth = member_sums(chosen, members)
    slope_oth, smooth_oth = member_sums(chosen, others)
    slope, smooth = slope + slope_oth, smooth + smooth_oth
    count_all = float(M)
    pairs_norm = count_all * (count_all - 1.0)
    to_truth = chosen - observed
    absolute = jnp.sqrt(to_truth * to_truth + smoothing * smoothing)
    gradient = weights * (to_truth / absolute / count_all - slope / pairs_norm)
    terms = weights * (absolute / count_all - (smooth - smoothing) / (2.0 * pairs_norm))
    return gradient.astype(bf16), terms


def all_to_all(x, axes):
    return lax.all_to_all(x, axes, 0, 0, tiled=True)


def copies(x, count):
    return jnp.broadcast_to(x[None], (count,) + x.shape)


def dot(a, b, ca, cb):
    return lax.dot_general(a, b, (((ca,), (cb,)), ((), ())), preferred_element_type=f32)


def body(latents, w_mix, w_out, bias, truth, area):
    first = lax.axis_index("c") == 0
    low = lax.axis_index("h") == 0
    points, width = latents.shape[1], latents.shape[2]
    fields = w_out.shape[1]
    rows = w_mix.shape[0]
    half = width // 2

    def pick(a, b):
        return jnp.where(first, a, b)

    mine = pick(w_mix[:, :half], w_mix[:, half:])
    far = lax.ppermute(mine, ("far", "h"), ACROSS)
    near = jnp.where(low, jnp.concatenate([mine, far], 0), jnp.concatenate([far, mine], 0))
    w_own = all_to_all(copies(near, Y * X), PLANE).reshape(width, half)
    out_own = pick(w_out.T[:, :half], w_out.T[:, half:])

    lat_own = latents[0]
    lat_oth = lax.ppermute(lat_own, "c", SWAP)
    pre_own = dot(lat_own, w_own, 1, 0)
    hid_own = jax.nn.gelu(pre_own).astype(bf16)
    pre_oth = dot(lat_oth, w_own, 1, 0)
    hid_oth = jax.nn.gelu(pre_oth).astype(bf16)

    like = jax.ShapeDtypeStruct
    part = call(
        forecast_kernel,
        like((2 * fields, points), f32),
        [out_own, hid_own, hid_oth],
        flops=4 * fields * points * half,
    )
    both = lax.all_gather(part, "c", axis=0)
    rest = pick(both[1], both[0])
    fc_own = part[:fields] + rest[fields:] + bias[:, None]
    fc_oth = part[fields:] + rest[:fields] + bias[:, None]
    members = all_to_all(copies(fc_own, Z), RING)
    both = lax.all_gather(members, "c", axis=0)
    others = pick(both[1], both[0])
    g_own, terms = pairwise(fc_own, members, others, truth, area)
    g_oth, unused_terms = pairwise(fc_oth, members, others, truth, area)

    gp_own, gp_oth, sent = call(
        backward_kernel,
        [
            like((points, half), bf16),
            like((points, half), bf16),
            like((Y * X, H * rows + 24, half), bf16),
        ],
        [g_own, g_oth, terms, out_own, pre_own, pre_oth, hid_own, hid_oth, lat_own, lat_oth],
        flops=4 * points * half * width,
    )
    got = all_to_all(sent, PLANE)

    piece, hpiece = rows // NEAR, fields // NEAR
    block = pltpu.VMEM((H * piece + 16, half), f32)
    gp_like = like((points, half), bf16)
    sent, gp_own, gp_oth = call(
        neighbour_kernel,
        [like((NEAR, H * piece + 16, half), bf16), gp_like, gp_like],
        [got, gp_own, gp_oth],
        [block],
        through=2,
    )
    got = all_to_all(sent, "near")
    block = pltpu.VMEM((16, half), f32)
    kernel = functools.partial(across_kernel, piece, hpiece)
    got = all_to_all(call(kernel, like((H * FAR, 16, half), bf16), [got], [block]), ("h", "far"))

    kernel = functools.partial(gather_kernel, piece, hpiece)
    sent = call(kernel, like((NEAR * CORES, 16, half), bf16), [got], [block])
    got = all_to_all(sent, ("near", "c"))
    rows_like, work = like((points, width), bf16), 16 * points * half * width
    grad_rows = call(partial_kernel, rows_like, [gp_oth, w_own], flops=work)
    grad_rows = lax.ppermute(grad_rows, "c", SWAP)
    grad_latents = call(latents_kernel, rows_like, [gp_own, w_own, grad_rows], flops=work)
    grad_mix, grad_out, grad_bias, loss, grad_latents = call(
        functools.partial(assemble_kernel, points * Y * X * H),
        [
            like((rows, width), f32),
            like((fields, width), f32),
            like((1, fields), f32),
            like((1, 1), f32),
            rows_like,
        ],
        [got, grad_latents],
        through=1,
    )
    return grad_latents[None], grad_mix, grad_out.T, grad_bias[0], loss[0, 0]


def solution(mesh):
    shape = (FAR, NEAR, CORES, Y, X, H)
    fine = Mesh(mesh.devices.reshape(shape), ("far", "near", "c", "y", "x", "h"))
    in_specs = (P(ENS, SPACE, None), P(SPACE, None), P(), P(), P(None, SPACE), P(SPACE))
    out_specs = (P(ENS, SPACE, None), P(SPACE, None), P(), P(), P())
    return jax.shard_map(
        body, mesh=fine, in_specs=in_specs, out_specs=out_specs, check_vma=False
    )
```

```python
import functools

import jax
import jax.numpy as jnp
from jax import lax
from jax.experimental import pallas as pl
from jax.experimental.pallas import tpu as pltpu
from jax.sharding import Mesh
from jax.sharding import PartitionSpec as P

M = 16
smoothing = 0.1
FAR, NEAR, CORES, Y, X, H = 2, 4, 2, 4, 4, 2
Z = FAR * NEAR
RING = ("far", "near")
ENS, SPACE, PLANE = ("far", "near", "c"), ("y", "x", "h"), ("y", "x")
f32, bf16 = jnp.float32, jnp.bfloat16
SWAP = ((0, 1), (1, 0))
ACROSS = tuple((far * H + h, (1 - far) * H + 1 - h) for far in range(FAR) for h in range(H))


LANES = 128


def split_row(values, width):
    first = values.astype(bf16).astype(f32)
    second = (values - first).astype(bf16).astype(f32)
    third = values - first - second
    return jnp.concatenate(
        [first, second, third, jnp.zeros((1, width - 3 * LANES), f32)], 1
    )


def joined_row(row):
    return row[:, :LANES] + row[:, LANES : 2 * LANES] + row[:, 2 * LANES : 3 * LANES]


def total(ref):
    result = ref[0].astype(f32)
    for k in range(1, ref.shape[0]):
        result = result + ref[k].astype(f32)
    return result


def call(kernel, shapes, operands, scratch=(), flops=0, through=0):
    vmem = pl.BlockSpec(memory_space=pltpu.VMEM)
    many = isinstance(shapes, list)
    size = sum(o.size * o.dtype.itemsize for o in operands)
    in_specs = [vmem] * len(operands)
    out_specs = [vmem] * len(shapes) if many else vmem
    aliases = {}
    for k in range(1, through + 1):
        in_specs[-k] = out_specs[-k] = pl.BlockSpec(memory_space=pl.ANY)
        aliases[len(operands) - k] = len(shapes) - k
    return pl.pallas_call(
        kernel,
        out_shape=shapes,
        in_specs=in_specs,
        out_specs=out_specs,
        input_output_aliases=aliases,
        scratch_shapes=list(scratch),
        compiler_params=pltpu.CompilerParams(vmem_limit_bytes=40 << 20),
        cost_estimate=pl.CostEstimate(flops=flops, bytes_accessed=size, transcendentals=0),
    )(*operands)


def gelu_slope(x):
    scale = 0.7978845608028654
    square = x * x
    t = jnp.tanh(scale * x * (1.0 + 0.044715 * square))
    return 0.5 * (1.0 + t) + (0.5 * scale) * x * (1.0 - t * t) * (1.0 + 0.134145 * square)


def repeat_kernel(block, sent):
    for k in range(sent.shape[0]):
        sent[k] = block[...]


def forecast_kernel(out, hid_own, hid_oth, part):
    fields = out.shape[0]
    part[:fields] = dot(out[...], hid_own[...], 1, 1)
    part[fields:] = dot(out[...], hid_oth[...], 1, 1)


def backward_kernel(
    g_own, g_oth, terms, out, pre_own, pre_oth, hid_own, hid_oth, lat_own, lat_oth,
    gp_own, gp_oth, sent,
):
    peers, rows = sent.shape[0], lat_own.shape[1] // sent.shape[0]
    fields, half = out.shape
    for g, pre, gp in ((g_own, pre_own, gp_own), (g_oth, pre_oth, gp_oth)):
        for k in range(0, pre.shape[0], 128):
            hidden = dot(g[:, k : k + 128], out[...], 0, 0)
            gp[k : k + 128] = (hidden * gelu_slope(pre[k : k + 128])).astype(bf16)
    head = dot(g_own[...], hid_own[...], 1, 0) + dot(g_oth[...], hid_oth[...], 1, 0)
    sums = jnp.sum(g_own[...].astype(f32), axis=1, keepdims=True)
    lane = lax.broadcasted_iota(jnp.int32, (fields, LANES), 1)
    field = lax.broadcasted_iota(jnp.int32, (fields, LANES), 0)
    values = jnp.sum(jnp.where(lane == field, sums, 0.0), axis=0, keepdims=True)
    loss = jnp.sum(jnp.sum(terms[...], axis=1, keepdims=True), axis=0, keepdims=True)
    values = jnp.where(lane[:1] == fields, loss, values)
    tail = jnp.where(
        lax.broadcasted_iota(jnp.int32, (8, half), 0) == 0, split_row(values, half), 0.0
    )
    step = 4
    for k in range(0, peers, step):
        columns = slice(k * rows, (k + step) * rows)
        mix = dot(lat_own[:, columns], gp_own[...], 0, 0)
        mix = mix + dot(lat_oth[:, columns], gp_oth[...], 0, 0)
        for j in range(step):
            block = [mix[j * rows : (j + 1) * rows], head, tail]
            sent[k + j] = jnp.concatenate(block, 0).astype(bf16)


def partial_kernel(gp, weight, rows):
    rows[...] = dot(gp[...], weight[...], 1, 1).astype(bf16)


def latents_kernel(gp, weight, other, rows):
    rows[...] = (dot(gp[...], weight[...], 1, 1) + other[...].astype(f32)).astype(bf16)


def pack(block, mix, head, values):
    start = 0
    for part in (*mix, head, split_row(values, block.shape[1])):
        block[start : start + part.shape[0]] = part
        start += part.shape[0]
    block[start:] = jnp.zeros((block.shape[0] - start, block.shape[1]), f32)
    return block[...].astype(bf16)


def neighbour_kernel(got, unused_a, unused_b, sent, unused_c, unused_d, block):
    rows, fields = got.shape[1] - 24, 16
    piece, hpiece = rows // H // NEAR, fields // NEAR
    whole = total(got)
    values = joined_row(whole[rows + fields : rows + fields + 1])
    for n in range(NEAR):
        mix = [
            whole[h * NEAR * piece + n * piece : h * NEAR * piece + (n + 1) * piece]
            for h in range(H)
        ]
        head = whole[rows + n * hpiece : rows + (n + 1) * hpiece]
        sent[n] = pack(block, mix, head, values)


def across_kernel(piece, hpiece, got, sent, block):
    whole = total(got)
    start = H * piece + hpiece
    values = joined_row(whole[start : start + 1])
    for h in range(H):
        mix = whole[h * piece : (h + 1) * piece]
        packed = pack(block, [mix], whole[H * piece : start], values)
        for far in range(FAR):
            sent[h * FAR + far] = packed


def gather_kernel(piece, hpiece, got, sent, block):
    whole = total(got)
    start = piece + hpiece
    values = joined_row(whole[start : start + 1])
    packed = pack(block, [whole[:piece]], whole[piece:start], values)
    for k in range(NEAR * CORES):
        sent[k] = packed


def assemble_kernel(count, got, unused_in, mix, head, bias, loss, unused_out):
    half = got.shape[2]
    piece, hpiece = mix.shape[0] // NEAR, head.shape[0] // NEAR
    for n in range(NEAR):
        for c in range(CORES):
            block = got[n * CORES + c].astype(f32)
            columns = slice(c * half, (c + 1) * half)
            mix[n * piece : (n + 1) * piece, columns] = block[:piece]
            head[n * hpiece : (n + 1) * hpiece, columns] = block[piece : piece + hpiece]
            if n == 0:
                row = joined_row(block[piece + hpiece : piece + hpiece + 1])
                values = row if c == 0 else values + row
    fields = head.shape[0]
    bias[...] = values[:, :fields]
    loss[...] = values[:, fields : fields + 1] / count


def member_sums(chosen, members):
    differ = chosen[None] - members
    smooth = jnp.sqrt(differ * differ + smoothing * smoothing)
    return jnp.sum(differ / smooth, axis=0), jnp.sum(smooth, axis=0)


def pairwise(chosen, members, others, observed, weights):
    slope, smooth = member_sums(chosen, members)
    slope_oth, smooth_oth = member_sums(chosen, others)
    slope, smooth = slope + slope_oth, smooth + smooth_oth
    count_all = float(M)
    pairs_norm = count_all * (count_all - 1.0)
    to_truth = chosen - observed
    absolute = jnp.sqrt(to_truth * to_truth + smoothing * smoothing)
    gradient = weights * (to_truth / absolute / count_all - slope / pairs_norm)
    terms = weights * (absolute / count_all - (smooth - smoothing) / (2.0 * pairs_norm))
    return gradient.astype(bf16), terms


def all_to_all(x, axes):
    return lax.all_to_all(x, axes, 0, 0, tiled=True)


def copies(x, count):
    return jnp.broadcast_to(x[None], (count,) + x.shape)


def dot(a, b, ca, cb):
    return lax.dot_general(a, b, (((ca,), (cb,)), ((), ())), preferred_element_type=f32)


def body(latents, w_mix, w_out, bias, truth, area):
    first = lax.axis_index("c") == 0
    low = lax.axis_index("h") == 0
    points, width = latents.shape[1], latents.shape[2]
    fields = w_out.shape[1]
    rows = w_mix.shape[0]
    half = width // 2

    def pick(a, b):
        return jnp.where(first, a, b)

    mine = pick(w_mix[:, :half], w_mix[:, half:])
    far = lax.ppermute(mine, ("far", "h"), ACROSS)
    near = jnp.where(low, jnp.concatenate([mine, far], 0), jnp.concatenate([far, mine], 0))
    sent = jax.ShapeDtypeStruct((Y * X, H * rows, half), bf16)
    w_own = all_to_all(call(repeat_kernel, sent, [near]), PLANE).reshape(width, half)
    out_own = pick(w_out.T[:, :half], w_out.T[:, half:])

    lat_own = latents[0]
    lat_oth = lax.ppermute(lat_own, "c", SWAP)
    pre_own = dot(lat_own, w_own, 1, 0)
    hid_own = jax.nn.gelu(pre_own).astype(bf16)
    pre_oth = dot(lat_oth, w_own, 1, 0)
    hid_oth = jax.nn.gelu(pre_oth).astype(bf16)

    like = jax.ShapeDtypeStruct
    part = call(
        forecast_kernel,
        like((2 * fields, points), f32),
        [out_own, hid_own, hid_oth],
        flops=4 * fields * points * half,
    )
    both = lax.all_gather(part, "c", axis=0)
    rest = pick(both[1], both[0])
    fc_own = part[:fields] + rest[fields:] + bias[:, None]
    fc_oth = part[fields:] + rest[:fields] + bias[:, None]
    members = all_to_all(copies(fc_own, Z), RING)
    both = lax.all_gather(members, "c", axis=0)
    others = pick(both[1], both[0])
    g_own, terms = pairwise(fc_own, members, others, truth, area)
    g_oth, unused_terms = pairwise(fc_oth, members, others, truth, area)

    gp_own, gp_oth, sent = call(
        backward_kernel,
        [
            like((points, half), bf16),
            like((points, half), bf16),
            like((Y * X, H * rows + 24, half), bf16),
        ],
        [g_own, g_oth, terms, out_own, pre_own, pre_oth, hid_own, hid_oth, lat_own, lat_oth],
        flops=4 * points * half * width,
    )
    got = all_to_all(sent, PLANE)

    piece, hpiece = rows // NEAR, fields // NEAR
    block = pltpu.VMEM((H * piece + 16, half), f32)
    gp_like = like((points, half), bf16)
    sent, gp_own, gp_oth = call(
        neighbour_kernel,
        [like((NEAR, H * piece + 16, half), bf16), gp_like, gp_like],
        [got, gp_own, gp_oth],
        [block],
        through=2,
    )
    got = all_to_all(sent, "near")
    block = pltpu.VMEM((16, half), f32)
    kernel = functools.partial(across_kernel, piece, hpiece)
    got = all_to_all(call(kernel, like((H * FAR, 16, half), bf16), [got], [block]), ("h", "far"))

    kernel = functools.partial(gather_kernel, piece, hpiece)
    sent = call(kernel, like((NEAR * CORES, 16, half), bf16), [got], [block])
    got = all_to_all(sent, ("near", "c"))
    rows_like, work = like((points, width), bf16), 16 * points * half * width
    grad_rows = call(partial_kernel, rows_like, [gp_oth, w_own], flops=work)
    grad_rows = lax.ppermute(grad_rows, "c", SWAP)
    grad_latents = call(latents_kernel, rows_like, [gp_own, w_own, grad_rows], flops=work)
    grad_mix, grad_out, grad_bias, loss, grad_latents = call(
        functools.partial(assemble_kernel, points * Y * X * H),
        [
            like((rows, width), f32),
            like((fields, width), f32),
            like((1, fields), f32),
            like((1, 1), f32),
            rows_like,
        ],
        [got, grad_latents],
        through=1,
    )
    return grad_latents[None], grad_mix, grad_out.T, grad_bias[0], loss[0, 0]


def solution(mesh):
    shape = (FAR, NEAR, CORES, Y, X, H)
    fine = Mesh(mesh.devices.reshape(shape), ("far", "near", "c", "y", "x", "h"))
    in_specs = (P(ENS, SPACE, None), P(SPACE, None), P(), P(), P(None, SPACE), P(SPACE))
    out_specs = (P(ENS, SPACE, None), P(SPACE, None), P(), P(), P())
    return jax.shard_map(
        body, mesh=fine, in_specs=in_specs, out_specs=out_specs, check_vma=False
    )
```
